32 devices in a mesh: dp: 8 (over y, x, core), ctx: 4 (over z).
Axes of the slice: x: 2, y: 2, z: 4, core: 2. Of those that a mesh axis runs over, the one named last changes fastest.
Arguments:
- queries: bfloat16 [8, 512, 2048], P('dp', 'ctx'), may hold values from -21 to 21
- keys: bfloat16 [8, 512, 512], P('dp', 'ctx'), may hold values from -21 to 21
- values: bfloat16 [8, 512, 512], P('dp', 'ctx'), may hold values from -6 to 6
- dout: bfloat16 [8, 512, 2048], P('dp', 'ctx'), may hold values from -6 to 6
- sinks: float32 [16], replicated, may hold values from 0 to 6
Outputs:
- grad_queries: bfloat16 [8, 512, 2048], P('dp', 'ctx')
- grad_keys: bfloat16 [8, 512, 512], P('dp', 'ctx')
- grad_values: bfloat16 [8, 512, 512], P('dp', 'ctx')
- sink_grad: float32 [16], replicated
The draws below stay inside these ranges and needn't reach their ends.
All inputs are finite; a program needn't handle non-finite values.
Results may differ from the reference program's by a relative error of at most 0.03.
Values may be sent and summed in bfloat16 or wider, within the bound.
No kernel may reach another device: no remote copies, remote signals or barrier semaphores. Data moves between devices by JAX's collectives and lax.ppermute only.
A program may use at most 64 MiB of HBM per device.

```python
import jax
import jax.numpy as jnp
from jax import lax

HEADS = 16
KV_HEADS = 4
HEAD = 128
WINDOW = 128
TOK_DEV = 128
BATCH = 8
LENGTH = 512


def draw_queries(key, part):
    drawn = jnp.clip(jax.random.normal(jax.random.fold_in(key, 21), (BATCH, LENGTH, HEADS * HEAD), jnp.float32), -4.0, 4.0)
    return drawn.astype(jnp.bfloat16)


def draw_keys(key, part):
    drawn = jnp.clip(jax.random.normal(jax.random.fold_in(key, 22), (BATCH, LENGTH, KV_HEADS * HEAD), jnp.float32), -4.0, 4.0)
    return drawn.astype(jnp.bfloat16)


def block_levels(rng, dims, shards, least, high):
    gain, own = 1.0, jax.random.fold_in(rng, 6)
    for dim, shards_of in shards:
        heights = jnp.exp(jax.random.uniform(jax.random.fold_in(own, dim), (shards_of,), jnp.float32, least / len(shards), high / len(shards)))
        gain = gain * jnp.repeat(heights, dims[dim] // shards_of).reshape([-1 if axis == dim else 1 for axis in range(len(dims))])
    return gain


def gaussian(key, dims, width, limit, cuts=(), kind=jnp.bfloat16):
    drawn = jax.random.normal(key, dims, jnp.float32) * width
    if len(cuts) > 0:
        drawn = block_levels(key, dims, cuts, -0.22, 0.18) * drawn
    return jnp.clip(drawn, min=-limit, max=limit).astype(kind)


def setup_inputs(seed: int = 0) -> dict:
    key_list = jax.random.split(jax.random.key(seed), 6)
    return {
        "queries": draw_queries(jax.random.fold_in(key_list[5], 71), 0),
        "keys": draw_keys(jax.random.fold_in(key_list[5], 71), 0),
        "values": gaussian(key_list[2], (BATCH, LENGTH, KV_HEADS * HEAD), 1.0, 6.0, ((0, 8), (1, 4))),
        "dout": gaussian(key_list[3], (BATCH, LENGTH, HEADS * HEAD), 1.0, 6.0, ((0, 8), (1, 4))),
        "sinks": jnp.clip(jax.random.uniform(key_list[4], (HEADS,), jnp.float32, 0.0, 6.0), 0.0, 6.0),
    }


def block_terms(query_rows, key_rows, value_rows, grad_rows, sinks, allowed):
    group_size = HEADS // KV_HEADS
    row_count = query_rows.shape[0]
    key_count = key_rows.shape[0]
    score_scale = HEAD ** (-0.5)
    key_mask = jnp.broadcast_to(allowed[:, None, :], (row_count, group_size, key_count)).reshape(row_count * group_size, key_count)
    grad_query_list = []
    grad_key_list = []
    grad_value_list = []
    sink_list = []
    for kv_head in range(KV_HEADS):
        low = kv_head * group_size * HEAD
        high = (kv_head + 1) * group_size * HEAD
        query_group = query_rows[:, low:high].reshape(row_count * group_size, HEAD)
        grad_group = grad_rows[:, low:high].reshape(row_count * group_size, HEAD)
        key_group = key_rows[:, kv_head * HEAD:(kv_head + 1) * HEAD]
        value_group = value_rows[:, kv_head * HEAD:(kv_head + 1) * HEAD]
        scores = lax.dot_general(query_group, key_group, (((1,), (1,)), ((), ())), preferred_element_type=jnp.float32) * score_scale
        sink_rows = jnp.tile(sinks[kv_head * group_size:(kv_head + 1) * group_size], row_count)
        row_max = jnp.maximum(lax.optimization_barrier(jnp.max(jnp.where(key_mask, scores, -jnp.inf), axis=1)), sink_rows)
        weights = jnp.where(key_mask, jnp.exp(scores - row_max[:, None]), 0.0)
        row_total = jnp.exp(sink_rows - row_max) + lax.optimization_barrier(jnp.sum(weights, axis=1))
        log_total = row_max + jnp.log(row_total)
        probabilities = jnp.where(key_mask, jnp.exp(scores - log_total[:, None]), 0.0)
        probs_low = probabilities.astype(jnp.bfloat16)
        attended = jnp.dot(probs_low, value_group, preferred_element_type=jnp.float32).astype(jnp.bfloat16)
        attended = lax.optimization_barrier(attended)
        row_delta = lax.optimization_barrier(jnp.sum(grad_group.astype(jnp.float32) * attended.astype(jnp.float32), axis=1))
        grad_prob = lax.dot_general(grad_group, value_group, (((1,), (1,)), ((), ())), preferred_element_type=jnp.float32)
        dscore = (probabilities * (grad_prob - row_delta[:, None])).astype(jnp.bfloat16)
        grad_query = jnp.dot(dscore, key_group, preferred_element_type=jnp.float32) * score_scale
        grad_query_list.append(grad_query.reshape(row_count, group_size * HEAD))
        grad_key_list.append(lax.dot_general(dscore, query_group, (((0,), (0,)), ((), ())), preferred_element_type=jnp.float32) * score_scale)
        grad_value_list.append(lax.dot_general(probs_low, grad_group, (((0,), (0,)), ((), ())), preferred_element_type=jnp.float32))
        sink_list.append(-lax.optimization_barrier(jnp.sum((jnp.exp(sink_rows - log_total) * row_delta).reshape(row_count, group_size), axis=0)))
    return (jnp.concatenate(grad_query_list, axis=1), jnp.concatenate(grad_key_list, axis=1), jnp.concatenate(grad_value_list, axis=1), jnp.concatenate(sink_list, axis=0))

def reference(queries, keys, values, dout, sinks):
    block_count = LENGTH // TOK_DEV

    def per_sequence(inputs):
        seq_queries, seq_keys, seq_values, seq_grads = inputs
        padding = jnp.zeros((WINDOW, seq_keys.shape[1]), seq_keys.dtype)
        keys_padded = jnp.concatenate([padding, seq_keys], axis=0)
        values_padded = jnp.concatenate([padding, seq_values], axis=0)

        def block_step(carried, block_index):
            key_acc, value_acc, sink_acc = carried
            block_start = (block_index * TOK_DEV).astype(jnp.int32)
            query_rows = lax.dynamic_slice_in_dim(seq_queries, block_start, TOK_DEV, 0)
            grad_rows = lax.dynamic_slice_in_dim(seq_grads, block_start, TOK_DEV, 0)
            key_rows = lax.dynamic_slice_in_dim(keys_padded, block_start, WINDOW + TOK_DEV, 0)
            value_rows = lax.dynamic_slice_in_dim(values_padded, block_start, WINDOW + TOK_DEV, 0)
            query_pos = block_start + jnp.arange(TOK_DEV, dtype=jnp.int32)
            key_pos = block_start - WINDOW + jnp.arange(WINDOW + TOK_DEV, dtype=jnp.int32)
            allowed = (key_pos[None, :] <= query_pos[:, None]) & (key_pos[None, :] > query_pos[:, None] - WINDOW) & (key_pos[None, :] >= 0)
            grad_query, grad_key, grad_value, sink_term = block_terms(query_rows, key_rows, value_rows, grad_rows, sinks, allowed)
            key_acc = lax.dynamic_update_slice_in_dim(key_acc, lax.dynamic_slice_in_dim(key_acc, block_start, WINDOW + TOK_DEV, 0) + grad_key, block_start, 0)
            value_acc = lax.dynamic_update_slice_in_dim(value_acc, lax.dynamic_slice_in_dim(value_acc, block_start, WINDOW + TOK_DEV, 0) + grad_value, block_start, 0)
            return ((key_acc, value_acc, sink_acc + sink_term), grad_query.astype(jnp.bfloat16))
        start_acc = jnp.zeros((WINDOW + LENGTH, KV_HEADS * HEAD), jnp.float32)
        carried, query_blocks = lax.scan(block_step, (start_acc, start_acc, jnp.zeros((HEADS,), jnp.float32)), jnp.arange(block_count, dtype=jnp.int32))
        key_acc, value_acc, sink_acc = carried
        return (query_blocks.reshape(LENGTH, HEADS * HEAD), key_acc[WINDOW:].astype(jnp.bfloat16), value_acc[WINDOW:].astype(jnp.bfloat16), sink_acc)
    grad_queries, grad_keys, grad_values, sink_terms = lax.map(per_sequence, (queries, keys, values, dout))
    sink_grad = lax.optimization_barrier(jnp.sum(sink_terms, axis=0)) / jnp.sqrt(jnp.float32(BATCH * LENGTH))
    return (grad_queries, grad_keys, grad_values, sink_grad)
```

```python
import functools

import jax
import jax.numpy as jnp
from jax import lax
from jax.experimental import pallas as pl
from jax.experimental.pallas import tpu as pltpu
from jax.sharding import PartitionSpec as P

HEADS = 16
KV_HEADS = 4
HEAD = 128
WINDOW = 128
GROUP = HEADS // KV_HEADS
SCALE = HEAD ** (-0.5)
LOG2E = 1.4426950408889634


def shifted(value, axis, steps):
    count = lax.axis_size(axis)
    leading, last = (max(0, -steps), min(count, count - steps))
    return lax.ppermute(value, axis, [(source, source + steps) for source in range(leading, last)])


def dot(a, b, dims):
    return lax.dot_general(a, b, (dims, ((), ())), preferred_element_type=jnp.float32)


def attention_kernel(first_ref, sinks_ref, q_ref, k_ref, v_ref, do_ref, hk_ref, hv_ref,
                     dq_ref, own_ref, back_ref, sink_ref):
    batch, rows, _ = q_ref.shape
    wide = GROUP * rows
    key_pos = lax.broadcasted_iota(jnp.int32, (rows, wide), 0)
    query_pos = lax.rem(lax.broadcasted_iota(jnp.int32, (rows, wide), 1), rows)
    own = key_pos <= query_pos
    bias = jnp.where(jnp.logical_and(first_ref[0] == 1, jnp.logical_not(own)), -1e30, 0.0)
    for b in range(batch):
        for g in range(KV_HEADS):
            kv = slice(g * HEAD, (g + 1) * HEAD)
            heads = range(g * GROUP, (g + 1) * GROUP)
            query = jnp.concatenate([q_ref[b, :, h * HEAD:(h + 1) * HEAD] for h in heads], axis=0)
            grad = jnp.concatenate([do_ref[b, :, h * HEAD:(h + 1) * HEAD] for h in heads], axis=0)
            key = jnp.concatenate([k_ref[b, :, kv], hk_ref[b, :, kv]], axis=0)
            value = jnp.concatenate([v_ref[b, :, kv], hv_ref[b, :, kv]], axis=0)
            scores = dot(key, query, ((1,), (1,)))
            grad_probs = dot(value, grad, ((1,), (1,)))
            score = jnp.where(own, scores[:rows], scores[rows:]) * (SCALE * LOG2E) + bias
            grad_prob = jnp.where(own, grad_probs[:rows], grad_probs[rows:])
            sink = jnp.concatenate(
                [jnp.full((1, rows), sinks_ref[h] * LOG2E, jnp.float32) for h in heads], axis=1)
            top = jnp.maximum(jnp.max(score, axis=0, keepdims=True), sink)
            weight = jnp.exp2(score - top)
            sink_weight = jnp.exp2(sink - top)
            scale = 1.0 / (jnp.sum(weight, axis=0, keepdims=True) + sink_weight)
            prob = weight * scale
            delta = jnp.sum(prob * grad_prob, axis=0, keepdims=True)
            dscore = prob * (grad_prob - delta)
            sink_term = sink_weight * scale * delta
            for n, h in enumerate(heads):
                term = sink_term[:, n * rows:(n + 1) * rows]
                if b == 0:
                    sink_ref[h:h + 1, :] = term
                else:
                    sink_ref[h:h + 1, :] += term
            zero = jnp.zeros_like(prob)
            probs = jnp.concatenate(
                [jnp.where(own, prob, zero), jnp.where(own, zero, prob)], axis=0).astype(jnp.bfloat16)
            dscores = jnp.concatenate(
                [jnp.where(own, dscore, zero), jnp.where(own, zero, dscore)], axis=0).astype(jnp.bfloat16)
            grad_key = dot(dscores, query, ((1,), (0,))) * SCALE
            grad_value = dot(probs, grad, ((1,), (0,)))
            grad_query = (dot(dscores, key, ((0,), (0,))) * SCALE).astype(jnp.bfloat16)
            for n, h in enumerate(heads):
                dq_ref[b, :, h * HEAD:(h + 1) * HEAD] = grad_query[n * rows:(n + 1) * rows]
            vcol = slice((KV_HEADS + g) * HEAD, (KV_HEADS + g + 1) * HEAD)
            own_ref[b, :, kv] = grad_key[:rows]
            own_ref[b, :, vcol] = grad_value[:rows]
            back_ref[b, :, kv] = grad_key[rows:].astype(jnp.bfloat16)
            back_ref[b, :, vcol] = grad_value[rows:].astype(jnp.bfloat16)


def attention(first, sinks, queries, keys, values, dout, halo_keys, halo_values):
    batch, rows, width = queries.shape
    kv_width = keys.shape[2]
    vmem = pl.BlockSpec(memory_space=pltpu.VMEM)
    smem = pl.BlockSpec(memory_space=pltpu.SMEM)
    return pl.pallas_call(
        attention_kernel,
        out_shape=(
            jax.ShapeDtypeStruct((batch, rows, width), jnp.bfloat16),
            jax.ShapeDtypeStruct((batch, rows, 2 * kv_width), jnp.float32),
            jax.ShapeDtypeStruct((batch, rows, 2 * kv_width), jnp.bfloat16),
            jax.ShapeDtypeStruct((HEADS, rows), jnp.float32),
        ),
        in_specs=[smem, smem] + [vmem] * 6,
        out_specs=(vmem,) * 4,
        compiler_params=pltpu.CompilerParams(vmem_limit_bytes=32 * 1024 * 1024),
        name="attention",
    )(first, sinks, queries, keys, values, dout, halo_keys, halo_values)


def total_over(value, axis):
    count = lax.axis_size(axis)
    if count & (count - 1):
        return lax.psum(value, axis)
    step = 1
    while step < count:
        value = value + lax.ppermute(value, axis, [(i, i ^ step) for i in range(count)])
        step *= 2
    return value


def body(queries, keys, values, dout, sinks):
    batch, rows, _ = queries.shape
    assert rows == WINDOW
    first = (lax.axis_index("ctx") == 0).astype(jnp.int32).reshape(1)
    halo_keys = shifted(keys, "ctx", 1)
    halo_values = shifted(values, "ctx", 1)
    grad_query, own, back, sink_terms = attention(
        first, sinks, queries, keys, values, dout, halo_keys, halo_values)
    arrived = shifted(back, "ctx", -1)
    total = total_over(total_over(sink_terms, "dp"), "ctx")
    joined = (own + arrived.astype(jnp.float32)).astype(jnp.bfloat16)
    kv_width = keys.shape[2]
    positions = lax.axis_size("dp") * batch * lax.axis_size("ctx") * rows
    sink_grad = -jnp.sum(total, axis=1) / jnp.sqrt(jnp.float32(positions))
    return grad_query, joined[:, :, :kv_width], joined[:, :, kv_width:], sink_grad


def solution(mesh):
    whole = P("dp", "ctx", None)
    return jax.shard_map(
        body,
        mesh=mesh,
        in_specs=(whole, whole, whole, whole, P()),
        out_specs=(whole, whole, whole, P()),
        check_vma=False,
    )
```

```python
import functools

import jax
import jax.numpy as jnp
from jax import lax
from jax.experimental import pallas as pl
from jax.experimental.pallas import tpu as pltpu
from jax.sharding import PartitionSpec as P

HEADS = 16
KV_HEADS = 4
HEAD = 128
WINDOW = 128
GROUP = HEADS // KV_HEADS
SCALE = HEAD ** (-0.5)
LOG2E = 1.4426950408889634
VMEM = pl.BlockSpec(memory_space=pltpu.VMEM)
SMEM = pl.BlockSpec(memory_space=pltpu.SMEM)
HBM = pl.BlockSpec(memory_space=pltpu.HBM)


def dot(a, b, dims):
    return lax.dot_general(a, b, (dims, ((), ())), preferred_element_type=jnp.float32)


def struct(shape, dtype):
    return jax.ShapeDtypeStruct(shape, dtype)


def call(kernel, name, out_shape, in_specs, args, flops, scratch=()):
    args = [
        pltpu.with_memory_space_constraint(a, pltpu.HBM) if spec is HBM else a
        for a, spec in zip(args, in_specs, strict=True)
    ]
    moved = sum(a.size * a.dtype.itemsize for a in (*args, *out_shape))
    return pl.pallas_call(
        kernel,
        out_shape=out_shape,
        in_specs=in_specs,
        out_specs=(VMEM,) * len(out_shape),
        scratch_shapes=scratch,
        compiler_params=pltpu.CompilerParams(vmem_limit_bytes=32 * 1024 * 1024),
        cost_estimate=pl.CostEstimate(flops=flops, bytes_accessed=moved, transcendentals=0),
        name=name,
    )(*args)


def own_mask(rows, width):
    key_pos = lax.broadcasted_iota(jnp.int32, (rows, width), 0)
    query_pos = lax.rem(lax.broadcasted_iota(jnp.int32, (rows, width), 1), rows)
    return key_pos <= query_pos


def stacked(ref, b, heads):
    return jnp.concatenate([ref[b, :, h * HEAD:(h + 1) * HEAD] for h in heads], axis=0)


def split(own, value):
    zero = jnp.zeros_like(value)
    return jnp.concatenate(
        [jnp.where(own, value, zero), jnp.where(own, zero, value)], axis=0).astype(jnp.bfloat16)


def groups(ref):
    batch, rows, _ = ref.shape
    for b in range(batch):
        for g in range(KV_HEADS):
            heads = range(g * GROUP, (g + 1) * GROUP)
            yield b, heads, slice(g * HEAD, (g + 1) * HEAD), slice(g * GROUP * rows, (g + 1) * GROUP * rows)


def load_kernel(first_ref, sinks_in, q_in, k_in, v_in, do_in,
                q_ref, k_ref, v_ref, do_ref, s_ref, dp_ref, bias_ref, sink_ref, sinks_ref, sems):
    _, rows, _ = q_ref.shape
    copies = [
        pltpu.make_async_copy(source, target, sems.at[n])
        for n, (source, target) in enumerate(
            ((k_in, k_ref), (q_in, q_ref), (v_in, v_ref), (do_in, do_ref), (sinks_in, sinks_ref)))
    ]
    for copy in copies:
        copy.start()
    bias_ref[...] = jnp.full(bias_ref.shape, jnp.where(first_ref[0] == 1, -1e30, 0.0), jnp.float32)
    copies[0].wait()
    copies[1].wait()
    for b, heads, kv, cols in groups(q_ref):
        s_ref[b, :, cols] = dot(k_ref[b, :, kv], stacked(q_ref, b, heads), ((1,), (1,)))
    copies[2].wait()
    copies[3].wait()
    for b, heads, kv, cols in groups(q_ref):
        dp_ref[b, :, cols] = dot(v_ref[b, :, kv], stacked(do_ref, b, heads), ((1,), (1,)))
    copies[4].wait()
    for h in range(HEADS):
        sink_ref[:, h * rows:(h + 1) * rows] = jnp.full((1, rows), sinks_ref[h] * LOG2E, jnp.float32)


def softmax_kernel(bias_ref, sink_ref, q_ref, hk_ref, s_ref, p_ref, sp_ref):
    _, rows, _ = q_ref.shape
    own = own_mask(rows, GROUP * rows)
    for b, heads, kv, cols in groups(q_ref):
        before = dot(hk_ref[b, :, kv], stacked(q_ref, b, heads), ((1,), (1,))) + bias_ref[...]
        score = jnp.where(own, s_ref[b, :, cols], before) * (SCALE * LOG2E)
        sink = sink_ref[:, cols]
        top = jnp.maximum(jnp.max(score, axis=0, keepdims=True), sink)
        weight = jnp.exp2(score - top)
        sink_weight = jnp.exp2(sink - top)
        scale = 1.0 / (jnp.sum(weight, axis=0, keepdims=True) + sink_weight)
        p_ref[b, :, cols] = weight * scale
        sp_ref[b, :, cols] = sink_weight * scale


def sink_kernel(do_ref, hv_ref, p_ref, sp_ref, dp_ref, gp_ref, delta_ref, sink_ref):
    _, rows, _ = do_ref.shape
    own = own_mask(rows, GROUP * rows)
    for b, heads, kv, cols in groups(do_ref):
        before = dot(hv_ref[b, :, kv], stacked(do_ref, b, heads), ((1,), (1,)))
        grad_prob = jnp.where(own, dp_ref[b, :, cols], before)
        gp_ref[b, :, cols] = grad_prob
        delta = jnp.sum(p_ref[b, :, cols] * grad_prob, axis=0, keepdims=True)
        delta_ref[b, :, cols] = delta
        terms = sp_ref[b, :, cols] * delta
        for n, h in enumerate(heads):
            term = terms[:, n * rows:(n + 1) * rows]
            if b == 0:
                sink_ref[h:h + 1, :] = term
            else:
                sink_ref[h:h + 1, :] += term


def grad_kernel(q_ref, do_ref, k_ref, hk_ref, p_ref, gp_ref, delta_ref, dq_ref, own_ref, back_ref):
    _, rows, _ = q_ref.shape
    width = KV_HEADS * HEAD
    own = own_mask(rows, GROUP * rows)
    for b, heads, kv, cols in groups(q_ref):
        prob = p_ref[b, :, cols]
        dscores = split(own, prob * (gp_ref[b, :, cols] - delta_ref[b, :, cols]))
        grad_key = dot(dscores, stacked(q_ref, b, heads), ((1,), (0,))) * SCALE
        grad_value = dot(split(own, prob), stacked(do_ref, b, heads), ((1,), (0,)))
        vcol = slice(width + kv.start, width + kv.stop)
        own_ref[b, :, kv] = grad_key[:rows]
        own_ref[b, :, vcol] = grad_value[:rows]
        back_ref[b, :, kv] = grad_key[rows:].astype(jnp.bfloat16)
        back_ref[b, :, vcol] = grad_value[rows:].astype(jnp.bfloat16)
        key = jnp.concatenate([k_ref[b, :, kv], hk_ref[b, :, kv]], axis=0)
        grad_query = (dot(dscores, key, ((0,), (0,))) * SCALE).astype(jnp.bfloat16)
        for n, h in enumerate(heads):
            dq_ref[b, :, h * HEAD:(h + 1) * HEAD] = grad_query[n * rows:(n + 1) * rows]


def finish_kernel(factor, own_ref, back_ref, total_ref, other_ref, dk_ref, dv_ref, sink_ref):
    width = dk_ref.shape[2]
    joined = (own_ref[...] + back_ref[...].astype(jnp.float32)).astype(jnp.bfloat16)
    dk_ref[...] = joined[:, :, :width]
    dv_ref[...] = joined[:, :, width:]
    total = total_ref[...] + other_ref[...]
    ones = jnp.ones((8, total.shape[1]), jnp.float32)
    sums = lax.dot_general(ones, total, (((1,), (1,)), ((), ())), precision=lax.Precision.HIGHEST,
                           preferred_element_type=jnp.float32)
    sink_ref[...] = sums[:1] * factor


def ring(value, axis, steps):
    count = lax.axis_size(axis)
    return lax.ppermute(value, axis, [(i, (i + steps) % count) for i in range(count)])


def exchange(value, over, across):
    dp, ctx = lax.axis_size("dp"), lax.axis_size("ctx")
    pairs = [(d * ctx + c, (d ^ over) * ctx + (c ^ across)) for d in range(dp) for c in range(ctx)]
    return lax.ppermute(value, ("dp", "ctx"), pairs)


def total_steps():
    dp, ctx = lax.axis_size("dp"), lax.axis_size("ctx")
    over = [1 << n for n in range(dp.bit_length() - 1)]
    across = [1 << n for n in range(ctx.bit_length() - 1)]
    cross = over[0] if over else 0
    return ([(over[0], 0)] if over else []) + [(cross, a) for a in reversed(across)] + [
        (cross | o, 0) for o in over[1:]]


def body(queries, keys, values, dout, sinks):
    batch, rows, width = queries.shape
    kv_width = keys.shape[2]
    dp, ctx = lax.axis_size("dp"), lax.axis_size("ctx")
    assert rows == WINDOW and dp & (dp - 1) == 0 and ctx & (ctx - 1) == 0
    bf16, f32 = jnp.bfloat16, jnp.float32
    square = struct((batch, rows, HEADS * rows), f32)
    line = struct((batch, 1, HEADS * rows), f32)
    kv_bf16 = struct((batch, rows, kv_width), bf16)
    product = 2 * batch * HEADS * rows * rows * HEAD

    first = (lax.axis_index("ctx") == 0).astype(jnp.int32).reshape(1)
    halo_keys = ring(keys, "ctx", 1)
    halo_values = ring(values, "ctx", 1)
    q, k, v, do, score, grad_prob, bias, sink = call(
        load_kernel, "load",
        (struct(queries.shape, bf16), kv_bf16, kv_bf16, struct(dout.shape, bf16), square, square,
         struct((1, GROUP * rows), f32), struct((1, HEADS * rows), f32)),
        [SMEM] + [HBM] * 5, (first, sinks, queries, keys, values, dout), 2 * product,
        scratch=[pltpu.SMEM((HEADS,), f32), pltpu.SemaphoreType.DMA((5,))])
    prob, sink_prob = call(
        softmax_kernel, "softmax", (square, line),
        [VMEM] * 5, (bias, sink, q, halo_keys, score), product)
    grad_prob, delta, total = call(
        sink_kernel, "sink", (square, line, struct((HEADS, rows), f32)),
        [VMEM] * 5, (do, halo_values, prob, sink_prob, grad_prob), product)
    grad_query, own, back = call(
        grad_kernel, "grad",
        (struct(queries.shape, bf16), struct((batch, rows, 2 * kv_width), f32),
         struct((batch, rows, 2 * kv_width), bf16)),
        [VMEM] * 7, (q, do, k, halo_keys, prob, grad_prob, delta), 6 * product)
    back = ring(back, "ctx", -1)
    *steps, last = total_steps()
    for over, across in steps:
        total = total + exchange(total, over, across)
    other = exchange(total, *last)
    factor = -1.0 / (dp * batch * ctx * rows) ** 0.5
    grad_keys, grad_values, sink_grad = call(
        functools.partial(finish_kernel, factor), "finish",
        (kv_bf16, kv_bf16, struct((1, HEADS), f32)),
        [VMEM] * 4, (own, back, total, other), 0)
    return grad_query, grad_keys, grad_values, sink_grad.reshape(HEADS)


def solution(mesh):
    whole = P("dp", "ctx", None)
    return jax.shard_map(
        body,
        mesh=mesh,
        in_specs=(whole, whole, whole, whole, P()),
        out_specs=(whole, whole, whole, P()),
        check_vma=False,
    )
```

```python
import functools

import jax
import jax.numpy as jnp
from jax import lax
from jax.experimental import pallas as pl
from jax.experimental.pallas import tpu as pltpu
from jax.sharding import PartitionSpec as P

HEADS = 16
KV_HEADS = 4
HEAD = 128
WINDOW = 128
GROUP = HEADS // KV_HEADS
SCALE = HEAD ** (-0.5)
LOG2E = 1.4426950408889634
VMEM = pl.BlockSpec(memory_space=pltpu.VMEM)
SMEM = pl.BlockSpec(memory_space=pltpu.SMEM)
ANY = pl.BlockSpec(memory_space=pl.ANY)
HBM = pl.BlockSpec(memory_space=pltpu.HBM)


def dot(a, b, dims):
    return lax.dot_general(a, b, (dims, ((), ())), preferred_element_type=jnp.float32)


def struct(shape, dtype):
    return jax.ShapeDtypeStruct(shape, dtype)


def call(kernel, name, out_shape, in_specs, args, flops, scratch=()):
    args = [
        pltpu.with_memory_space_constraint(a, pltpu.HBM) if spec is HBM else a
        for a, spec in zip(args, in_specs, strict=True)
    ]
    moved = sum(a.size * a.dtype.itemsize for a in (*args, *out_shape))
    return pl.pallas_call(
        kernel,
        out_shape=out_shape,
        in_specs=in_specs,
        out_specs=(VMEM,) * len(out_shape),
        scratch_shapes=scratch,
        compiler_params=pltpu.CompilerParams(vmem_limit_bytes=32 * 1024 * 1024),
        cost_estimate=pl.CostEstimate(flops=flops, bytes_accessed=moved, transcendentals=0),
        name=name,
    )(*args)


def own_mask(rows, width):
    key_pos = lax.broadcasted_iota(jnp.int32, (rows, width), 0)
    query_pos = lax.rem(lax.broadcasted_iota(jnp.int32, (rows, width), 1), rows)
    return key_pos <= query_pos


def stacked(ref, b, heads):
    return jnp.concatenate([ref[b, :, h * HEAD:(h + 1) * HEAD] for h in heads], axis=0)


def split(own, value):
    zero = jnp.zeros_like(value)
    return jnp.concatenate(
        [jnp.where(own, value, zero), jnp.where(own, zero, value)], axis=0).astype(jnp.bfloat16)


def groups(ref):
    batch, rows, _ = ref.shape
    for b in range(batch):
        for g in range(KV_HEADS):
            heads = range(g * GROUP, (g + 1) * GROUP)
            yield b, heads, slice(g * HEAD, (g + 1) * HEAD), slice(g * GROUP * rows, (g + 1) * GROUP * rows)


def load_kernel(first_ref, sinks_in, q_in, k_in, v_in, do_in,
                q_ref, k_ref, v_ref, do_ref, s_ref, dp_ref, bias_ref, sink_ref, sinks_ref, sems):
    _, rows, _ = q_ref.shape
    copies = [
        pltpu.make_async_copy(source, target, sems.at[n])
        for n, (source, target) in enumerate(
            ((k_in, k_ref), (q_in, q_ref), (v_in, v_ref), (do_in, do_ref), (sinks_in, sinks_ref)))
    ]
    for copy in copies:
        copy.start()
    bias_ref[...] = jnp.full(bias_ref.shape, jnp.where(first_ref[0] == 1, -1e30, 0.0), jnp.float32)
    copies[0].wait()
    copies[1].wait()
    for b, heads, kv, cols in groups(q_ref):
        s_ref[b, :, cols] = dot(k_ref[b, :, kv], stacked(q_ref, b, heads), ((1,), (1,)))
    copies[2].wait()
    copies[3].wait()
    for b, heads, kv, cols in groups(q_ref):
        dp_ref[b, :, cols] = dot(v_ref[b, :, kv], stacked(do_ref, b, heads), ((1,), (1,)))
    copies[4].wait()
    for h in range(HEADS):
        sink_ref[:, h * rows:(h + 1) * rows] = jnp.full((1, rows), sinks_ref[h] * LOG2E, jnp.float32)


def softmax_kernel(bias_ref, sink_ref, q_ref, hk_ref, s_ref, p_ref, sp_ref):
    _, rows, _ = q_ref.shape
    own = own_mask(rows, GROUP * rows)
    for b, heads, kv, cols in groups(q_ref):
        before = dot(hk_ref[b, :, kv], stacked(q_ref, b, heads), ((1,), (1,))) + bias_ref[...]
        score = jnp.where(own, s_ref[b, :, cols], before) * (SCALE * LOG2E)
        sink = sink_ref[:, cols]
        top = jnp.maximum(jnp.max(score, axis=0, keepdims=True), sink)
        weight = jnp.exp2(score - top)
        sink_weight = jnp.exp2(sink - top)
        scale = 1.0 / (jnp.sum(weight, axis=0, keepdims=True) + sink_weight)
        p_ref[b, :, cols] = weight * scale
        sp_ref[b, :, cols] = sink_weight * scale


def sink_kernel(do_ref, hv_ref, p_ref, sp_ref, dp_ref, gp_ref, delta_ref, sink_ref):
    _, rows, _ = do_ref.shape
    own = own_mask(rows, GROUP * rows)
    for b, heads, kv, cols in groups(do_ref):
        before = dot(hv_ref[b, :, kv], stacked(do_ref, b, heads), ((1,), (1,)))
        grad_prob = jnp.where(own, dp_ref[b, :, cols], before)
        gp_ref[b, :, cols] = grad_prob
        delta = jnp.sum(p_ref[b, :, cols] * grad_prob, axis=0, keepdims=True)
        delta_ref[b, :, cols] = delta
        terms = sp_ref[b, :, cols] * delta
        for n, h in enumerate(heads):
            term = terms[:, n * rows:(n + 1) * rows]
            if b == 0:
                sink_ref[h:h + 1, :] = term
            else:
                sink_ref[h:h + 1, :] += term


def grad_kernel(q_ref, do_ref, k_ref, hk_ref, p_ref, gp_ref, delta_ref, dq_ref, own_ref, back_ref):
    _, rows, _ = q_ref.shape
    width = KV_HEADS * HEAD
    own = own_mask(rows, GROUP * rows)
    for b, heads, kv, cols in groups(q_ref):
        prob = p_ref[b, :, cols]
        dscores = split(own, prob * (gp_ref[b, :, cols] - delta_ref[b, :, cols]))
        grad_key = dot(dscores, stacked(q_ref, b, heads), ((1,), (0,))) * SCALE
        grad_value = dot(split(own, prob), stacked(do_ref, b, heads), ((1,), (0,)))
        vcol = slice(width + kv.start, width + kv.stop)
        own_ref[b, :, kv] = grad_key[:rows]
        own_ref[b, :, vcol] = grad_value[:rows]
        back_ref[b, :, kv] = grad_key[rows:].astype(jnp.bfloat16)
        back_ref[b, :, vcol] = grad_value[rows:].astype(jnp.bfloat16)
        key = jnp.concatenate([k_ref[b, :, kv], hk_ref[b, :, kv]], axis=0)
        grad_query = (dot(dscores, key, ((0,), (0,))) * SCALE).astype(jnp.bfloat16)
        for n, h in enumerate(heads):
            dq_ref[b, :, h * HEAD:(h + 1) * HEAD] = grad_query[n * rows:(n + 1) * rows]


def add_kernel(a_ref, b_ref, *refs):
    refs[-1][...] = a_ref[...] + b_ref[...]


def finish_kernel(factor, own_ref, back_ref, total_ref, other_ref, dk_ref, dv_ref, sink_ref):
    width = dk_ref.shape[2]
    joined = (own_ref[...] + back_ref[...].astype(jnp.float32)).astype(jnp.bfloat16)
    dk_ref[...] = joined[:, :, :width]
    dv_ref[...] = joined[:, :, width:]
    total = total_ref[...] + other_ref[...]
    ones = jnp.ones((8, total.shape[1]), jnp.float32)
    sums = lax.dot_general(ones, total, (((1,), (1,)), ((), ())), precision=lax.Precision.HIGHEST,
                           preferred_element_type=jnp.float32)
    sink_ref[...] = sums[:1] * factor


def ring(value, axis, steps):
    count = lax.axis_size(axis)
    return lax.ppermute(value, axis, [(i, (i + steps) % count) for i in range(count)])


def exchange(value, over, across):
    dp, ctx = lax.axis_size("dp"), lax.axis_size("ctx")
    pairs = [(d * ctx + c, (d ^ over) * ctx + (c ^ across)) for d in range(dp) for c in range(ctx)]
    return lax.ppermute(value, ("dp", "ctx"), pairs)


def total_steps():
    dp, ctx = lax.axis_size("dp"), lax.axis_size("ctx")
    over = [1 << n for n in range(dp.bit_length() - 1)]
    across = [1 << n for n in range(ctx.bit_length() - 1)]
    cross = over[0] if over else 0
    return ([(over[0], 0)] if over else []) + [(cross, a) for a in reversed(across)] + [
        (cross | o, 0) for o in over[1:]]


def body(queries, keys, values, dout, sinks):
    batch, rows, width = queries.shape
    kv_width = keys.shape[2]
    dp, ctx = lax.axis_size("dp"), lax.axis_size("ctx")
    assert rows == WINDOW and dp & (dp - 1) == 0 and ctx & (ctx - 1) == 0
    bf16, f32 = jnp.bfloat16, jnp.float32
    square = struct((batch, rows, HEADS * rows), f32)
    line = struct((batch, 1, HEADS * rows), f32)
    kv_bf16 = struct((batch, rows, kv_width), bf16)
    product = 2 * batch * HEADS * rows * rows * HEAD

    first = (lax.axis_index("ctx") == 0).astype(jnp.int32).reshape(1)
    halo_keys = ring(keys, "ctx", 1)
    halo_values = ring(values, "ctx", 1)
    q, k, v, do, score, grad_prob, bias, sink = call(
        load_kernel, "load",
        (struct(queries.shape, bf16), kv_bf16, kv_bf16, struct(dout.shape, bf16), square, square,
         struct((1, GROUP * rows), f32), struct((1, HEADS * rows), f32)),
        [SMEM] + [HBM] * 5, (first, sinks, queries, keys, values, dout), 2 * product,
        scratch=[pltpu.SMEM((HEADS,), f32), pltpu.SemaphoreType.DMA((5,))])
    prob, sink_prob = call(
        softmax_kernel, "softmax", (square, line),
        [VMEM] * 5, (bias, sink, q, halo_keys, score), product)
    grad_prob, delta, total = call(
        sink_kernel, "sink", (square, line, struct((HEADS, rows), f32)),
        [VMEM] * 5, (do, halo_values, prob, sink_prob, grad_prob), product)
    grad_query, own, back = call(
        grad_kernel, "grad",
        (struct(queries.shape, bf16), struct((batch, rows, 2 * kv_width), f32),
         struct((batch, rows, 2 * kv_width), bf16)),
        [VMEM] * 7, (q, do, k, halo_keys, prob, grad_prob, delta), 6 * product)
    token = back
    back = ring(back, "ctx", -1)
    *steps, last = total_steps()
    for n, (over, across) in enumerate(steps):
        received = exchange(total, over, across)
        if n == 1:
            total, = call(add_kernel, "add", (struct(total.shape, f32),), [VMEM] * 2 + [ANY], (total, received, token), 0)
        elif n == 2:
            total, = call(add_kernel, "add", (struct(total.shape, f32),), [VMEM] * 2, (total, received), 10 ** 10)
        else:
            total = total + received
    other = exchange(total, *last)
    factor = -1.0 / (dp * batch * ctx * rows) ** 0.5
    grad_keys, grad_values, sink_grad = call(
        functools.partial(finish_kernel, factor), "finish",
        (kv_bf16, kv_bf16, struct((1, HEADS), f32)),
        [VMEM] * 4, (own, back, total, other), 0)
    return grad_query, grad_keys, grad_values, sink_grad.reshape(HEADS)


def solution(mesh):
    whole = P("dp", "ctx", None)
    return jax.shard_map(
        body,
        mesh=mesh,
        in_specs=(whole, whole, whole, whole, P()),
        out_specs=(whole, whole, whole, P()),
        check_vma=False,
    )
```

```python
import functools
import math

import jax
import jax.numpy as jnp
from jax import lax
from jax.experimental import pallas as pl
from jax.experimental.pallas import tpu as pltpu
from jax.sharding import PartitionSpec as P

HEADS = 16
KV_HEADS = 4
HEAD = 128
WINDOW = 128
GROUP = HEADS // KV_HEADS
SCALE = HEAD ** (-0.5)
LOG2E = 1.4426950408889634
VMEM = pl.BlockSpec(memory_space=pltpu.VMEM)
SMEM = pl.BlockSpec(memory_space=pltpu.SMEM)
ANY = pl.BlockSpec(memory_space=pl.ANY)
HBM = pl.BlockSpec(memory_space=pltpu.HBM)


def dot(a, b, dims):
    return lax.dot_general(a, b, (dims, ((), ())), preferred_element_type=jnp.float32)


def struct(shape, dtype):
    return jax.ShapeDtypeStruct(shape, dtype)


def call(kernel, name, out_shape, in_specs, args, flops, scratch=(), out_specs=None):
    args = [
        pltpu.with_memory_space_constraint(a, pltpu.HBM) if spec is HBM else a
        for a, spec in zip(args, in_specs, strict=True)
    ]
    moved = sum(math.prod(a.shape) * a.dtype.itemsize for a in (*args, *out_shape))
    return pl.pallas_call(
        kernel,
        out_shape=out_shape,
        in_specs=in_specs,
        out_specs=out_specs or (VMEM,) * len(out_shape),
        scratch_shapes=scratch,
        compiler_params=pltpu.CompilerParams(vmem_limit_bytes=32 * 1024 * 1024),
        cost_estimate=pl.CostEstimate(flops=flops, bytes_accessed=moved, transcendentals=0),
        name=name,
    )(*args)


def own_mask(rows, width):
    key_pos = lax.broadcasted_iota(jnp.int32, (rows, width), 0)
    query_pos = lax.rem(lax.broadcasted_iota(jnp.int32, (rows, width), 1), rows)
    return key_pos <= query_pos


def stacked(ref, b, heads):
    return jnp.concatenate([ref[b, :, h * HEAD:(h + 1) * HEAD] for h in heads], axis=0)


def split(own, value):
    zero = jnp.zeros_like(value)
    return jnp.concatenate(
        [jnp.where(own, value, zero), jnp.where(own, zero, value)], axis=0).astype(jnp.bfloat16)


def groups(ref):
    batch, rows, _ = ref.shape
    for b in range(batch):
        for g in range(KV_HEADS):
            heads = range(g * GROUP, (g + 1) * GROUP)
            yield b, heads, slice(g * HEAD, (g + 1) * HEAD), slice(g * GROUP * rows, (g + 1) * GROUP * rows)


def load_kernel(first_ref, sinks_in, q_in, k_in, v_in, do_in,
                q_ref, k_ref, v_ref, do_ref, s_ref, dp_ref, bias_ref, sink_ref, sinks_ref, sems):
    _, rows, _ = q_ref.shape
    copies = [
        pltpu.make_async_copy(source, target, sems.at[n])
        for n, (source, target) in enumerate(
            ((k_in, k_ref), (q_in, q_ref), (v_in, v_ref), (do_in, do_ref), (sinks_in, sinks_ref)))
    ]
    for copy in copies:
        copy.start()
    bias_ref[...] = jnp.full(bias_ref.shape, jnp.where(first_ref[0] == 1, -1e30, 0.0), jnp.float32)
    copies[0].wait()
    copies[1].wait()
    for b, heads, kv, cols in groups(q_ref):
        s_ref[b, :, cols] = dot(k_ref[b, :, kv], stacked(q_ref, b, heads), ((1,), (1,)))
    copies[2].wait()
    copies[3].wait()
    for b, heads, kv, cols in groups(q_ref):
        dp_ref[b, :, cols] = dot(v_ref[b, :, kv], stacked(do_ref, b, heads), ((1,), (1,)))
    copies[4].wait()
    for h in range(HEADS):
        sink_ref[:, h * rows:(h + 1) * rows] = jnp.full((1, rows), sinks_ref[h] * LOG2E, jnp.float32)


def softmax_kernel(bias_ref, sink_ref, q_ref, do_ref, hk_ref, s_ref, p_ref, sp_ref, dv_ref, back_ref):
    _, rows, _ = q_ref.shape
    own = own_mask(rows, GROUP * rows)
    for b, heads, kv, cols in groups(q_ref):
        before = dot(hk_ref[b, :, kv], stacked(q_ref, b, heads), ((1,), (1,))) + bias_ref[...]
        score = jnp.where(own, s_ref[b, :, cols], before) * (SCALE * LOG2E)
        sink = sink_ref[:, cols]
        top = jnp.maximum(jnp.max(score, axis=0, keepdims=True), sink)
        weight = jnp.exp2(score - top)
        sink_weight = jnp.exp2(sink - top)
        scale = 1.0 / (jnp.sum(weight, axis=0, keepdims=True) + sink_weight)
        prob = weight * scale
        p_ref[b, :, cols] = prob
        sp_ref[b, :, cols] = sink_weight * scale
        grad_value = dot(split(own, prob), stacked(do_ref, b, heads), ((1,), (0,)))
        dv_ref[b, :, kv] = grad_value[:rows]
        back_ref[b, :, kv] = grad_value[rows:].astype(jnp.bfloat16)


def grad_kernel(q_ref, do_ref, k_ref, hk_ref, hv_ref, p_ref, sp_ref, dp_ref, back_dv_ref,
                terms_out, dq_ref, dk_ref, back_ref, gp_ref, delta_ref, sink_ref, terms_ref, sem):
    _, rows, _ = q_ref.shape
    width = KV_HEADS * HEAD
    own = own_mask(rows, GROUP * rows)
    sink_ref[...] = jnp.zeros_like(sink_ref)
    for b, heads, kv, cols in groups(do_ref):
        before = dot(hv_ref[b, :, kv], stacked(do_ref, b, heads), ((1,), (1,)))
        grad_prob = jnp.where(own, dp_ref[b, :, cols], before)
        gp_ref[b, :, cols] = grad_prob
        delta = jnp.sum(p_ref[b, :, cols] * grad_prob, axis=0, keepdims=True)
        delta_ref[b, :, cols] = delta
        terms = sp_ref[b, :, cols] * delta
        for n, h in enumerate(heads):
            sink_ref[h:h + 1, :] += terms[:, n * rows:(n + 1) * rows]
    ones = jnp.ones((terms_ref.shape[0], rows), jnp.bfloat16)
    terms = sink_ref[...]
    high = terms.astype(jnp.bfloat16)
    rest = terms - high.astype(jnp.float32)
    middle = rest.astype(jnp.bfloat16)
    low = (rest - middle.astype(jnp.float32)).astype(jnp.bfloat16)
    terms_ref[...] = sum(dot(ones, part, ((1,), (1,))) for part in (low, middle, high))
    copy = pltpu.make_async_copy(terms_ref, terms_out, sem)
    copy.start()
    back_ref[:, :, width:] = back_dv_ref[...]
    for b, heads, kv, cols in groups(q_ref):
        dscores = split(own, p_ref[b, :, cols] * (gp_ref[b, :, cols] - delta_ref[b, :, cols]))
        grad_key = dot(dscores, stacked(q_ref, b, heads), ((1,), (0,))) * SCALE
        dk_ref[b, :, kv] = grad_key[:rows]
        back_ref[b, :, kv] = grad_key[rows:].astype(jnp.bfloat16)
        key = jnp.concatenate([k_ref[b, :, kv], hk_ref[b, :, kv]], axis=0)
        grad_query = (dot(dscores, key, ((0,), (0,))) * SCALE).astype(jnp.bfloat16)
        for n, h in enumerate(heads):
            dq_ref[b, :, h * HEAD:(h + 1) * HEAD] = grad_query[n * rows:(n + 1) * rows]
    copy.wait()


def finish_kernel(factor, own_dk_ref, own_dv_ref, back_ref, terms_ref, dk_ref, dv_ref, sink_ref):
    width = dk_ref.shape[2]
    dk_ref[...] = (own_dk_ref[...] + back_ref[:, :, :width].astype(jnp.float32)).astype(jnp.bfloat16)
    dv_ref[...] = (own_dv_ref[...] + back_ref[:, :, width:].astype(jnp.float32)).astype(jnp.bfloat16)
    sink_ref[...] = jnp.sum(terms_ref[...], axis=0, keepdims=True)[:, :HEADS] * factor


def ring(value, axis, steps):
    count = lax.axis_size(axis)
    return lax.ppermute(value, axis, [(i, (i + steps) % count) for i in range(count)])


def shift(value, axis):
    count = lax.axis_size(axis)
    return lax.ppermute(value, axis, [(i, i + 1) for i in range(count - 1)])


def body(queries, keys, values, dout, sinks):
    batch, rows, width = queries.shape
    kv_width = keys.shape[2]
    dp, ctx = lax.axis_size("dp"), lax.axis_size("ctx")
    assert rows == WINDOW and dp & (dp - 1) == 0 and ctx & (ctx - 1) == 0
    bf16, f32 = jnp.bfloat16, jnp.float32
    square = struct((batch, rows, HEADS * rows), f32)
    line = struct((batch, 1, HEADS * rows), f32)
    kv_bf16 = struct((batch, rows, kv_width), bf16)
    kv_f32 = struct((batch, rows, kv_width), f32)
    product = 2 * batch * HEADS * rows * rows * HEAD

    first = (lax.axis_index("ctx") == 0).astype(jnp.int32).reshape(1)
    halo_keys = ring(keys, "ctx", 1)
    halo_values = shift(values, "ctx")
    q, k, v, do, score, grad_prob, bias, sink = call(
        load_kernel, "load",
        (struct(queries.shape, bf16), kv_bf16, kv_bf16, struct(dout.shape, bf16), square, square,
         struct((1, GROUP * rows), f32), struct((1, HEADS * rows), f32)),
        [SMEM] + [HBM] * 5, (first, sinks, queries, keys, values, dout), 2 * product,
        scratch=[pltpu.SMEM((HEADS,), f32), pltpu.SemaphoreType.DMA((5,))])
    prob, sink_prob, own_values, back_values = call(
        softmax_kernel, "softmax", (square, line, kv_f32, kv_bf16),
        [VMEM] * 6, (bias, sink, q, do, halo_keys, score), 3 * product)
    terms, grad_query, own_keys, back = call(
        grad_kernel, "grad",
        (struct((dp * ctx, HEADS), f32), pltpu.VMEM(queries.shape, bf16), kv_f32,
         struct((batch, rows, 2 * kv_width), bf16)),
        [VMEM] * 9, (q, do, k, halo_keys, halo_values, prob, sink_prob, grad_prob, back_values), 5 * product,
        scratch=[pltpu.VMEM(square.shape, f32), pltpu.VMEM(line.shape, f32), pltpu.VMEM((HEADS, rows), f32),
                 pltpu.VMEM((dp * ctx, HEADS), f32), pltpu.SemaphoreType.DMA],
        out_specs=(HBM, VMEM, VMEM, VMEM))
    back = ring(back, "ctx", -1)
    terms = lax.all_to_all(terms, ("dp", "ctx"), 0, 0, tiled=True)
    factor = -1.0 / (dp * batch * ctx * rows) ** 0.5
    grad_keys, grad_values, sink_grad = call(
        functools.partial(finish_kernel, factor), "finish",
        (kv_bf16, kv_bf16, struct((1, HEADS), f32)),
        [VMEM] * 4, (own_keys, own_values, back, terms), 0)
    return grad_query, grad_keys, grad_values, sink_grad.reshape(HEADS)


def solution(mesh):
    whole = P("dp", "ctx", None)
    return jax.shard_map(
        body,
        mesh=mesh,
        in_specs=(whole, whole, whole, whole, P()),
        out_specs=(whole, whole, whole, P()),
        check_vma=False,
    )
```

```python
import functools
import math

import jax
import jax.numpy as jnp
from jax import lax
from jax.experimental import pallas as pl
from jax.experimental.pallas import tpu as pltpu
from jax.sharding import PartitionSpec as P

HEADS = 16
KV_HEADS = 4
HEAD = 128
WINDOW = 128
GROUP = HEADS // KV_HEADS
SCALE = HEAD ** (-0.5)
LOG2E = 1.4426950408889634
VMEM = pl.BlockSpec(memory_space=pltpu.VMEM)
SMEM = pl.BlockSpec(memory_space=pltpu.SMEM)
ANY = pl.BlockSpec(memory_space=pl.ANY)
HBM = pl.BlockSpec(memory_space=pltpu.HBM)


def dot(a, b, dims):
    return lax.dot_general(a, b, (dims, ((), ())), preferred_element_type=jnp.float32)


def struct(shape, dtype):
    return jax.ShapeDtypeStruct(shape, dtype)


def call(kernel, name, out_shape, in_specs, args, flops, scratch=(), out_specs=None):
    args = [
        pltpu.with_memory_space_constraint(a, pltpu.HBM) if spec is HBM else a
        for a, spec in zip(args, in_specs, strict=True)
    ]
    moved = sum(math.prod(a.shape) * a.dtype.itemsize for a in (*args, *out_shape))
    return pl.pallas_call(
        kernel,
        out_shape=out_shape,
        in_specs=in_specs,
        out_specs=out_specs or (VMEM,) * len(out_shape),
        scratch_shapes=scratch,
        compiler_params=pltpu.CompilerParams(vmem_limit_bytes=32 * 1024 * 1024),
        cost_estimate=pl.CostEstimate(flops=flops, bytes_accessed=moved, transcendentals=0),
        name=name,
    )(*args)


def own_mask(rows, width):
    key_pos = lax.broadcasted_iota(jnp.int32, (rows, width), 0)
    query_pos = lax.rem(lax.broadcasted_iota(jnp.int32, (rows, width), 1), rows)
    return key_pos <= query_pos


def stacked(ref, b, heads):
    return jnp.concatenate([ref[b, :, h * HEAD:(h + 1) * HEAD] for h in heads], axis=0)


def split(own, value):
    zero = jnp.zeros_like(value)
    return jnp.concatenate(
        [jnp.where(own, value, zero), jnp.where(own, zero, value)], axis=0).astype(jnp.bfloat16)


def groups(ref):
    batch, rows, _ = ref.shape
    for b in range(batch):
        for g in range(KV_HEADS):
            heads = range(g * GROUP, (g + 1) * GROUP)
            yield b, heads, slice(g * HEAD, (g + 1) * HEAD), slice(g * GROUP * rows, (g + 1) * GROUP * rows)


def load_kernel(first_ref, sinks_in, q_in, k_in, v_in, do_in,
                q_ref, k_ref, v_ref, do_ref, s_ref, dp_ref, bias_ref, sink_ref, sinks_ref, sems):
    _, rows, _ = q_ref.shape
    copies = [
        pltpu.make_async_copy(source, target, sems.at[n])
        for n, (source, target) in enumerate(
            ((k_in, k_ref), (q_in, q_ref), (v_in, v_ref), (do_in, do_ref), (sinks_in, sinks_ref)))
    ]
    for copy in copies:
        copy.start()
    bias_ref[...] = jnp.full(bias_ref.shape, jnp.where(first_ref[0] == 1, -1e30, 0.0), jnp.float32)
    copies[0].wait()
    copies[1].wait()
    for b, heads, kv, cols in groups(q_ref):
        s_ref[b, :, cols] = dot(k_ref[b, :, kv], stacked(q_ref, b, heads), ((1,), (1,)))
    copies[2].wait()
    copies[3].wait()
    for b, heads, kv, cols in groups(q_ref):
        dp_ref[b, :, cols] = dot(v_ref[b, :, kv], stacked(do_ref, b, heads), ((1,), (1,)))
    copies[4].wait()
    for h in range(HEADS):
        sink_ref[:, h * rows:(h + 1) * rows] = jnp.full((1, rows), sinks_ref[h] * LOG2E, jnp.float32)


def softmax_kernel(bias_ref, sink_ref, q_ref, do_ref, hk_ref, s_ref, p_ref, sp_ref, dv_ref, back_ref):
    _, rows, _ = q_ref.shape
    own = own_mask(rows, GROUP * rows)
    for b, heads, kv, cols in groups(q_ref):
        before = dot(hk_ref[b, :, kv], stacked(q_ref, b, heads), ((1,), (1,))) + bias_ref[...]
        score = jnp.where(own, s_ref[b, :, cols], before) * (SCALE * LOG2E)
        sink = sink_ref[:, cols]
        top = jnp.maximum(jnp.max(score, axis=0, keepdims=True), sink)
        weight = jnp.exp2(score - top)
        sink_weight = jnp.exp2(sink - top)
        scale = 1.0 / (jnp.sum(weight, axis=0, keepdims=True) + sink_weight)
        prob = weight * scale
        p_ref[b, :, cols] = prob
        sp_ref[b, :, cols] = sink_weight * scale
        grad_value = dot(split(own, prob), stacked(do_ref, b, heads), ((1,), (0,)))
        dv_ref[b, :, kv] = grad_value[:rows]
        back_ref[b, :, kv] = grad_value[rows:].astype(jnp.bfloat16)


def grad_kernel(q_ref, do_ref, k_ref, hk_ref, hv_ref, p_ref, sp_ref, dp_ref,
                terms_out, dq_ref, dk_ref, back_ref, gp_ref, delta_ref, sink_ref, terms_ref, sem):
    _, rows, _ = q_ref.shape
    own = own_mask(rows, GROUP * rows)
    sink_ref[...] = jnp.zeros_like(sink_ref)
    for b, heads, kv, cols in groups(do_ref):
        before = dot(hv_ref[b, :, kv], stacked(do_ref, b, heads), ((1,), (1,)))
        grad_prob = jnp.where(own, dp_ref[b, :, cols], before)
        gp_ref[b, :, cols] = grad_prob
        delta = jnp.sum(p_ref[b, :, cols] * grad_prob, axis=0, keepdims=True)
        delta_ref[b, :, cols] = delta
        terms = sp_ref[b, :, cols] * delta
        for n, h in enumerate(heads):
            sink_ref[h:h + 1, :] += terms[:, n * rows:(n + 1) * rows]
    ones = jnp.ones((terms_ref.shape[0], rows), jnp.bfloat16)
    terms = sink_ref[...]
    high = terms.astype(jnp.bfloat16)
    rest = terms - high.astype(jnp.float32)
    middle = rest.astype(jnp.bfloat16)
    low = (rest - middle.astype(jnp.float32)).astype(jnp.bfloat16)
    terms_ref[...] = sum(dot(ones, part, ((1,), (1,))) for part in (low, middle, high))
    copy = pltpu.make_async_copy(terms_ref, terms_out, sem)
    copy.start()
    for b, heads, kv, cols in groups(q_ref):
        dscores = split(own, p_ref[b, :, cols] * (gp_ref[b, :, cols] - delta_ref[b, :, cols]))
        grad_key = dot(dscores, stacked(q_ref, b, heads), ((1,), (0,))) * SCALE
        dk_ref[b, :, kv] = grad_key[:rows]
        back_ref[b, :, kv] = grad_key[rows:].astype(jnp.bfloat16)
        key = jnp.concatenate([k_ref[b, :, kv], hk_ref[b, :, kv]], axis=0)
        grad_query = (dot(dscores, key, ((0,), (0,))) * SCALE).astype(jnp.bfloat16)
        for n, h in enumerate(heads):
            dq_ref[b, :, h * HEAD:(h + 1) * HEAD] = grad_query[n * rows:(n + 1) * rows]
    copy.wait()


def join_kernel(own_ref, back_ref, out_ref):
    out_ref[...] = (own_ref[...] + back_ref[...].astype(jnp.float32)).astype(jnp.bfloat16)


def total_kernel(factor, terms_ref, _, total_ref):
    total_ref[...] = jnp.sum(terms_ref[...], axis=0, keepdims=True) * factor


def finish_kernel(own_ref, back_ref, total_ref, out_ref, sink_ref):
    join_kernel(own_ref, back_ref, out_ref)
    sink_ref[...] = total_ref[...]


def ring(value, axis, steps):
    count = lax.axis_size(axis)
    return lax.ppermute(value, axis, [(i, (i + steps) % count) for i in range(count)])


def shift(value, axis):
    count = lax.axis_size(axis)
    return lax.ppermute(value, axis, [(i, i + 1) for i in range(count - 1)])


def body(queries, keys, values, dout, sinks):
    batch, rows, width = queries.shape
    kv_width = keys.shape[2]
    dp, ctx = lax.axis_size("dp"), lax.axis_size("ctx")
    assert rows == WINDOW and dp & (dp - 1) == 0 and ctx & (ctx - 1) == 0
    bf16, f32 = jnp.bfloat16, jnp.float32
    square = struct((batch, rows, HEADS * rows), f32)
    line = struct((batch, 1, HEADS * rows), f32)
    kv_bf16 = struct((batch, rows, kv_width), bf16)
    product = 2 * batch * HEADS * rows * rows * HEAD

    first = (lax.axis_index("ctx") == 0).astype(jnp.int32).reshape(1)
    halo_keys = ring(keys, "ctx", 1)
    halo_values = shift(values, "ctx")
    q, k, v, do, score, grad_prob, bias, sink = call(
        load_kernel, "load",
        (struct(queries.shape, bf16), kv_bf16, kv_bf16, struct(dout.shape, bf16), square, square,
         struct((1, GROUP * rows), f32), struct((1, HEADS * rows), f32)),
        [SMEM] + [HBM] * 5, (first, sinks, queries, keys, values, dout), 2 * product,
        scratch=[pltpu.SMEM((HEADS,), f32), pltpu.SemaphoreType.DMA((5,))])
    prob, sink_prob, own_values, back_values = call(
        softmax_kernel, "softmax",
        (pltpu.VMEM(square.shape, f32), pltpu.VMEM(line.shape, f32), pltpu.VMEM(keys.shape, f32),
         pltpu.VMEM(keys.shape, bf16)),
        [VMEM] * 6, (bias, sink, q, do, halo_keys, score), 3 * product)
    back_values = ring(back_values, "ctx", -1)
    terms, grad_query, own_keys, back_keys = call(
        grad_kernel, "grad",
        (struct((dp * ctx, HEADS), f32), pltpu.VMEM(queries.shape, bf16), pltpu.VMEM(keys.shape, f32),
         pltpu.VMEM(keys.shape, bf16)),
        [VMEM] * 8, (q, do, k, halo_keys, halo_values, prob, sink_prob, grad_prob), 5 * product,
        scratch=[pltpu.VMEM(square.shape, f32), pltpu.VMEM(line.shape, f32), pltpu.VMEM((HEADS, rows), f32),
                 pltpu.VMEM((dp * ctx, HEADS), f32), pltpu.SemaphoreType.DMA],
        out_specs=(HBM, VMEM, VMEM, VMEM))
    back_keys = ring(back_keys, "ctx", -1)
    terms = lax.all_to_all(terms, ("dp", "ctx"), 0, 0, tiled=True)
    grad_values, = call(join_kernel, "join", (kv_bf16,), [VMEM] * 2, (own_values, back_values), 0)
    factor = -1.0 / (dp * batch * ctx * rows) ** 0.5
    total, = call(
        functools.partial(total_kernel, factor), "total", (struct((1, HEADS), f32),), [VMEM, HBM],
        (terms, grad_values), 10 ** 10)
    grad_keys, sink_grad = call(
        finish_kernel, "finish", (kv_bf16, struct((1, HEADS), f32)), [VMEM] * 3, (own_keys, back_keys, total), 0)
    return grad_query, grad_keys, grad_values, sink_grad.reshape(HEADS)


def solution(mesh):
    whole = P("dp", "ctx", None)
    return jax.shard_map(
        body,
        mesh=mesh,
        in_specs=(whole, whole, whole, whole, P()),
        out_specs=(whole, whole, whole, P()),
        check_vma=False,
    )
```

```python
import functools
import math

import jax
import jax.numpy as jnp
from jax import lax
from jax.experimental import pallas as pl
from jax.experimental.pallas import tpu as pltpu
from jax.sharding import PartitionSpec as P

HEADS = 16
KV_HEADS = 4
HEAD = 128
WINDOW = 128
GROUP = HEADS // KV_HEADS
SCALE = HEAD ** (-0.5)
LOG2E = 1.4426950408889634
VMEM = pl.BlockSpec(memory_space=pltpu.VMEM)
SMEM = pl.BlockSpec(memory_space=pltpu.SMEM)
ANY = pl.BlockSpec(memory_space=pl.ANY)
HBM = pl.BlockSpec(memory_space=pltpu.HBM)


def dot(a, b, dims):
    return lax.dot_general(a, b, (dims, ((), ())), preferred_element_type=jnp.float32)


def struct(shape, dtype):
    return jax.ShapeDtypeStruct(shape, dtype)


def call(kernel, name, out_shape, in_specs, args, flops, scratch=(), out_specs=None):
    args = [
        pltpu.with_memory_space_constraint(a, pltpu.HBM) if spec is HBM else a
        for a, spec in zip(args, in_specs, strict=True)
    ]
    moved = sum(math.prod(a.shape) * a.dtype.itemsize for a in (*args, *out_shape))
    return pl.pallas_call(
        kernel,
        out_shape=out_shape,
        in_specs=in_specs,
        out_specs=out_specs or (VMEM,) * len(out_shape),
        scratch_shapes=scratch,
        compiler_params=pltpu.CompilerParams(vmem_limit_bytes=32 * 1024 * 1024),
        cost_estimate=pl.CostEstimate(flops=flops, bytes_accessed=moved, transcendentals=0),
        name=name,
    )(*args)


def own_mask(rows, width):
    key_pos = lax.broadcasted_iota(jnp.int32, (rows, width), 0)
    query_pos = lax.rem(lax.broadcasted_iota(jnp.int32, (rows, width), 1), rows)
    return key_pos <= query_pos


def stacked(ref, b, heads):
    return jnp.concatenate([ref[b, :, h * HEAD:(h + 1) * HEAD] for h in heads], axis=0)


def split(own, value):
    value = value.astype(jnp.bfloat16)
    part = value * own.astype(jnp.float32).astype(jnp.bfloat16)
    return jnp.concatenate([part, value - part], axis=0)


def groups(ref):
    batch, rows, _ = ref.shape
    for b in range(batch):
        for g in range(KV_HEADS):
            heads = range(g * GROUP, (g + 1) * GROUP)
            yield b, heads, slice(g * HEAD, (g + 1) * HEAD), slice(g * GROUP * rows, (g + 1) * GROUP * rows)


def load_kernel(first_ref, sinks_in, q_in, k_in, v_in, do_in,
                q_ref, k_ref, v_ref, do_ref, s_ref, dp_ref, bias_ref, sink_ref, sinks_ref, sems):
    _, rows, _ = q_ref.shape
    copies = [
        pltpu.make_async_copy(source, target, sems.at[n])
        for n, (source, target) in enumerate(
            ((k_in, k_ref), (q_in, q_ref), (v_in, v_ref), (do_in, do_ref), (sinks_in, sinks_ref)))
    ]
    for copy in copies:
        copy.start()
    bias_ref[...] = jnp.full(bias_ref.shape, jnp.where(first_ref[0] == 1, -1e30, 0.0), jnp.float32)
    copies[0].wait()
    copies[1].wait()
    for b, heads, kv, cols in groups(q_ref):
        s_ref[b, :, cols] = dot(k_ref[b, :, kv], stacked(q_ref, b, heads), ((1,), (1,)))
    copies[2].wait()
    copies[3].wait()
    for b, heads, kv, cols in groups(q_ref):
        dp_ref[b, :, cols] = dot(v_ref[b, :, kv], stacked(do_ref, b, heads), ((1,), (1,)))
    copies[4].wait()
    for h in range(HEADS):
        sink_ref[:, h * rows:(h + 1) * rows] = jnp.full((1, rows), sinks_ref[h] * LOG2E, jnp.float32)


def softmax_kernel(bias_ref, sink_ref, q_ref, do_ref, hk_ref, s_ref, p_ref, sp_ref, dv_ref, back_ref):
    _, rows, _ = q_ref.shape
    own = own_mask(rows, GROUP * rows)
    parts = list(groups(q_ref))
    for b, heads, kv, cols in parts:
        before = dot(hk_ref[b, :, kv], stacked(q_ref, b, heads), ((1,), (1,))) + bias_ref[...]
        p_ref[b, :, cols] = jnp.where(own, s_ref[b, :, cols], before) * (SCALE * LOG2E)
    tops = [jnp.maximum(jnp.max(p_ref[b, :, cols], axis=0, keepdims=True), sink_ref[:, cols])
            for b, _, _, cols in parts]
    sums = []
    for (b, _, _, cols), top in zip(parts, tops):
        weight = jnp.exp2(p_ref[b, :, cols] - top)
        p_ref[b, :, cols] = weight
        sums.append(jnp.sum(weight, axis=0, keepdims=True))
    scales = []
    for (b, _, _, cols), top, total in zip(parts, tops, sums):
        sink_weight = jnp.exp2(sink_ref[:, cols] - top)
        scales.append(1.0 / (total + sink_weight))
        sp_ref[b, :, cols] = sink_weight * scales[-1]
    probs = []
    for (b, _, _, cols), scale in zip(parts, scales):
        prob = p_ref[b, :, cols] * scale
        p_ref[b, :, cols] = prob
        probs.append(split(own, prob))
    for (b, heads, kv, cols), prob in zip(parts, probs):
        grad_value = dot(prob, stacked(do_ref, b, heads), ((1,), (0,)))
        dv_ref[b, :, kv] = grad_value[:rows]
        back_ref[b, :, kv] = grad_value[rows:].astype(jnp.bfloat16)


def grad_kernel(q_ref, do_ref, hv_ref, p_ref, sp_ref, dp_ref,
                terms_out, ds_ref, dk_ref, back_ref, gp_ref, sink_ref, terms_ref, sem):
    _, rows, _ = q_ref.shape
    own = own_mask(rows, GROUP * rows)
    parts = list(groups(q_ref))
    for b, heads, kv, cols in parts:
        before = dot(hv_ref[b, :, kv], stacked(do_ref, b, heads), ((1,), (1,)))
        gp_ref[b, :, cols] = jnp.where(own, dp_ref[b, :, cols], before)
    deltas = [jnp.sum(p_ref[b, :, cols] * gp_ref[b, :, cols], axis=0, keepdims=True) for b, _, _, cols in parts]
    for (b, heads, _, cols), delta in zip(parts, deltas):
        terms = sp_ref[b, :, cols] * delta
        for n, h in enumerate(heads):
            term = terms[:, n * rows:(n + 1) * rows]
            sink_ref[h:h + 1, :] = term if b == 0 else sink_ref[h:h + 1, :] + term
    terms = sink_ref[...]
    high = terms.astype(jnp.bfloat16)
    rest = terms - high.astype(jnp.float32)
    middle = rest.astype(jnp.bfloat16)
    low = (rest - middle.astype(jnp.float32)).astype(jnp.bfloat16)
    split_terms = jnp.concatenate([low, middle, high], axis=1)
    ones = jnp.ones((terms_ref.shape[0], split_terms.shape[1]), jnp.bfloat16)
    terms_ref[...] = dot(ones, split_terms, ((1,), (1,)))
    copy = pltpu.make_async_copy(terms_ref, terms_out, sem)
    copy.start()
    for (b, _, _, cols), delta in zip(parts, deltas):
        ds_ref[b, :, cols] = split(own, p_ref[b, :, cols] * (gp_ref[b, :, cols] - delta))
    for b, heads, kv, cols in parts:
        grad_key = dot(ds_ref[b, :, cols], stacked(q_ref, b, heads), ((1,), (0,))) * SCALE
        dk_ref[b, :, kv] = grad_key[:rows]
        back_ref[b, :, kv] = grad_key[rows:].astype(jnp.bfloat16)
    copy.wait()


def query_kernel(k_ref, hk_ref, ds_ref, dq_ref):
    _, rows, _ = dq_ref.shape
    parts = list(groups(dq_ref))
    keys = [jnp.concatenate([k_ref[b, :, kv], hk_ref[b, :, kv]], axis=0) for b, _, kv, _ in parts]
    products = [dot(ds_ref[b, :, cols], key, ((0,), (0,))) for (b, _, _, cols), key in zip(parts, keys)]
    for (b, heads, _, _), product in zip(parts, products):
        for n, h in enumerate(heads):
            dq_ref[b, :, h * HEAD:(h + 1) * HEAD] = (product[n * rows:(n + 1) * rows] * SCALE).astype(jnp.bfloat16)


def join_kernel(own_ref, back_ref, out_ref):
    out_ref[...] = (own_ref[...] + back_ref[...].astype(jnp.float32)).astype(jnp.bfloat16)


def total_kernel(factor, terms_ref, *refs):
    total_ref = refs[-1]
    total_ref[...] = jnp.sum(terms_ref[...], axis=0, keepdims=True) * factor


def finish_kernel(own_ref, back_ref, total_ref, out_ref, sink_ref):
    join_kernel(own_ref, back_ref, out_ref)
    sink_ref[...] = total_ref[...]


def ring(value, axis, steps):
    count = lax.axis_size(axis)
    return lax.ppermute(value, axis, [(i, (i + steps) % count) for i in range(count)])


def shift(value, axis):
    count = lax.axis_size(axis)
    return lax.ppermute(value, axis, [(i, i + 1) for i in range(count - 1)])


def body(queries, keys, values, dout, sinks):
    batch, rows, width = queries.shape
    kv_width = keys.shape[2]
    dp, ctx = lax.axis_size("dp"), lax.axis_size("ctx")
    assert rows == WINDOW and dp & (dp - 1) == 0 and ctx & (ctx - 1) == 0
    bf16, f32 = jnp.bfloat16, jnp.float32
    square = struct((batch, rows, HEADS * rows), f32)
    line = struct((batch, 1, HEADS * rows), f32)
    kv_bf16 = struct((batch, rows, kv_width), bf16)
    product = 2 * batch * HEADS * rows * rows * HEAD

    first = (lax.axis_index("ctx") == 0).astype(jnp.int32).reshape(1)
    halo_keys = ring(keys, "ctx", 1)
    halo_values = shift(values, "ctx")
    q, k, v, do, score, grad_prob, bias, sink = call(
        load_kernel, "load",
        (struct(queries.shape, bf16), kv_bf16, kv_bf16, struct(dout.shape, bf16), square, square,
         struct((1, GROUP * rows), f32), struct((1, HEADS * rows), f32)),
        [SMEM] + [HBM] * 5, (first, sinks, queries, keys, values, dout), 2 * product,
        scratch=[pltpu.SMEM((HEADS,), f32), pltpu.SemaphoreType.DMA((5,))])
    prob, sink_prob, own_values, back_values = call(
        softmax_kernel, "softmax",
        (pltpu.VMEM(square.shape, f32), pltpu.VMEM(line.shape, f32), pltpu.VMEM(keys.shape, f32),
         pltpu.VMEM(keys.shape, bf16)),
        [VMEM] * 6, (bias, sink, q, do, halo_keys, score), 3 * product)
    back_values = ring(back_values, "ctx", -1)
    terms, dscores, own_keys, back_keys = call(
        grad_kernel, "grad",
        (struct((dp * ctx, HEADS), f32), pltpu.VMEM((batch, 2 * rows, HEADS * rows), bf16), pltpu.VMEM(keys.shape, f32),
         pltpu.VMEM(keys.shape, bf16)),
        [VMEM] * 6, (q, do, halo_values, prob, sink_prob, grad_prob), 3 * product,
        scratch=[pltpu.VMEM(square.shape, f32), pltpu.VMEM((HEADS, rows), f32),
                 pltpu.VMEM((dp * ctx, HEADS), f32), pltpu.SemaphoreType.DMA],
        out_specs=(HBM, VMEM, VMEM, VMEM))
    back_keys = ring(back_keys, "ctx", -1)
    terms = lax.all_to_all(terms, ("dp", "ctx"), 0, 0, tiled=True)
    grad_query, = call(query_kernel, "query", (struct(queries.shape, bf16),), [VMEM] * 3, (k, halo_keys, dscores), 2 * product)
    grad_values, = call(join_kernel, "join", (kv_bf16,), [VMEM] * 2, (own_values, back_values), 0)
    factor = -1.0 / (dp * batch * ctx * rows) ** 0.5
    total, = call(
        functools.partial(total_kernel, factor), "total", (struct((1, HEADS), f32),), [VMEM, HBM, HBM],
        (terms, grad_values, grad_query), 10 ** 10)
    grad_keys, sink_grad = call(
        finish_kernel, "finish", (kv_bf16, struct((1, HEADS), f32)), [VMEM] * 3, (own_keys, back_keys, total), 0)
    return grad_query, grad_keys, grad_values, sink_grad.reshape(HEADS)


def solution(mesh):
    whole = P("dp", "ctx", None)
    return jax.shard_map(
        body,
        mesh=mesh,
        in_specs=(whole, whole, whole, whole, P()),
        out_specs=(whole, whole, whole, P()),
        check_vma=False,
    )
```

```python
import functools
import math

import jax
import jax.numpy as jnp
from jax import lax
from jax.experimental import pallas as pl
from jax.experimental.pallas import tpu as pltpu
from jax.sharding import PartitionSpec as P

HEADS = 16
KV_HEADS = 4
HEAD = 128
WINDOW = 128
GROUP = HEADS // KV_HEADS
SCALE = HEAD ** (-0.5)
LOG2E = 1.4426950408889634
VMEM = pl.BlockSpec(memory_space=pltpu.VMEM)
SMEM = pl.BlockSpec(memory_space=pltpu.SMEM)
HBM = pl.BlockSpec(memory_space=pltpu.HBM)


def dot(a, b, dims):
    return lax.dot_general(a, b, (dims, ((), ())), preferred_element_type=jnp.float32)


def struct(shape, dtype):
    return jax.ShapeDtypeStruct(shape, dtype)


def call(kernel, name, out_shape, in_specs, args, flops, scratch=(), out_specs=None):
    args = [
        pltpu.with_memory_space_constraint(a, pltpu.HBM) if spec is HBM else a
        for a, spec in zip(args, in_specs, strict=True)
    ]
    moved = sum(math.prod(a.shape) * a.dtype.itemsize for a in (*args, *out_shape))
    return pl.pallas_call(
        kernel,
        out_shape=out_shape,
        in_specs=in_specs,
        out_specs=out_specs or (VMEM,) * len(out_shape),
        scratch_shapes=scratch,
        compiler_params=pltpu.CompilerParams(vmem_limit_bytes=32 * 1024 * 1024),
        cost_estimate=pl.CostEstimate(flops=flops, bytes_accessed=moved, transcendentals=0),
        name=name,
    )(*args)


def own_mask(rows, width):
    key_pos = lax.broadcasted_iota(jnp.int32, (rows, width), 0)
    query_pos = lax.rem(lax.broadcasted_iota(jnp.int32, (rows, width), 1), rows)
    return key_pos <= query_pos


def stacked(ref, b, heads):
    return jnp.concatenate([ref[b, :, h * HEAD:(h + 1) * HEAD] for h in heads], axis=0)


def split(own, value):
    value = value.astype(jnp.bfloat16)
    part = value * own.astype(jnp.float32).astype(jnp.bfloat16)
    return jnp.concatenate([part, value - part], axis=0)


def groups(ref):
    batch, rows, _ = ref.shape
    for b in range(batch):
        for g in range(KV_HEADS):
            heads = range(g * GROUP, (g + 1) * GROUP)
            yield b, heads, slice(g * HEAD, (g + 1) * HEAD), slice(g * GROUP * rows, (g + 1) * GROUP * rows)


def load_kernel(first_ref, sinks_in, q_in, k_in, v_in, do_in,
                q_ref, k_ref, do_ref, s_ref, dp_ref, bias_ref, sink_ref, v_ref, sinks_ref, sems):
    _, rows, _ = q_ref.shape
    copies = [
        pltpu.make_async_copy(source, target, sems.at[n])
        for n, (source, target) in enumerate(
            ((k_in, k_ref), (q_in, q_ref), (v_in, v_ref), (do_in, do_ref), (sinks_in, sinks_ref)))
    ]
    for copy in copies:
        copy.start()
    bias_ref[...] = jnp.full(bias_ref.shape, jnp.where(first_ref[0] == 1, -1e30, 0.0), jnp.float32)
    copies[0].wait()
    copies[1].wait()
    for b, heads, kv, cols in groups(q_ref):
        s_ref[b, :, cols] = dot(k_ref[b, :, kv], stacked(q_ref, b, heads), ((1,), (1,)))
    copies[2].wait()
    copies[3].wait()
    for b, heads, kv, cols in groups(q_ref):
        dp_ref[b, :, cols] = dot(v_ref[b, :, kv], stacked(do_ref, b, heads), ((1,), (1,)))
    copies[4].wait()
    for h in range(HEADS):
        sink_ref[:, h * rows:(h + 1) * rows] = jnp.full((1, rows), sinks_ref[h] * LOG2E, jnp.float32)


def softmax_kernel(bias_ref, sink_ref, q_ref, do_ref, hk_ref, s_ref, p_ref, sp_ref, dv_ref, back_ref):
    _, rows, _ = q_ref.shape
    own = own_mask(rows, GROUP * rows)
    parts = list(groups(q_ref))
    for b, heads, kv, cols in parts:
        before = dot(hk_ref[b, :, kv], stacked(q_ref, b, heads), ((1,), (1,))) + bias_ref[...]
        p_ref[b, :, cols] = jnp.where(own, s_ref[b, :, cols], before) * (SCALE * LOG2E)
    tops = [jnp.maximum(jnp.max(p_ref[b, :, cols], axis=0, keepdims=True), sink_ref[:, cols])
            for b, _, _, cols in parts]
    sums = []
    for (b, _, _, cols), top in zip(parts, tops):
        weight = jnp.exp2(p_ref[b, :, cols] - top)
        p_ref[b, :, cols] = weight
        sums.append(jnp.sum(weight, axis=0, keepdims=True))
    scales = []
    for (b, _, _, cols), top, total in zip(parts, tops, sums):
        sink_weight = jnp.exp2(sink_ref[:, cols] - top)
        scales.append(1.0 / (total + sink_weight))
        sp_ref[b, :, cols] = sink_weight * scales[-1]
    probs = []
    for (b, _, _, cols), scale in zip(parts, scales):
        prob = p_ref[b, :, cols] * scale
        p_ref[b, :, cols] = prob
        probs.append(split(own, prob))
    for (b, heads, kv, cols), prob in zip(parts, probs):
        grad_value = dot(prob, stacked(do_ref, b, heads), ((1,), (0,)))
        dv_ref[b, :, kv] = grad_value[:rows]
        back_ref[b, :, kv] = grad_value[rows:].astype(jnp.bfloat16)


def grad_kernel(q_ref, do_ref, hv_ref, p_ref, sp_ref, dp_ref,
                terms_out, ds_ref, dk_ref, back_ref, gp_ref, sink_ref, terms_ref, sem):
    _, rows, _ = q_ref.shape
    own = own_mask(rows, GROUP * rows)
    parts = list(groups(q_ref))
    for b, heads, kv, cols in parts:
        before = dot(hv_ref[b, :, kv], stacked(do_ref, b, heads), ((1,), (1,)))
        gp_ref[b, :, cols] = jnp.where(own, dp_ref[b, :, cols], before)
    deltas = [jnp.sum(p_ref[b, :, cols] * gp_ref[b, :, cols], axis=0, keepdims=True) for b, _, _, cols in parts]
    for (b, heads, _, cols), delta in zip(parts, deltas):
        terms = sp_ref[b, :, cols] * delta
        for n, h in enumerate(heads):
            term = terms[:, n * rows:(n + 1) * rows]
            sink_ref[h:h + 1, :] = term if b == 0 else sink_ref[h:h + 1, :] + term
    terms = sink_ref[...]
    high = terms.astype(jnp.bfloat16)
    rest = terms - high.astype(jnp.float32)
    middle = rest.astype(jnp.bfloat16)
    low = (rest - middle.astype(jnp.float32)).astype(jnp.bfloat16)
    split_terms = jnp.concatenate([low, middle, high], axis=1)
    ones = jnp.ones((terms_ref.shape[0], split_terms.shape[1]), jnp.bfloat16)
    terms_ref[...] = dot(ones, split_terms, ((1,), (1,)))
    copy = pltpu.make_async_copy(terms_ref, terms_out, sem)
    copy.start()
    for (b, _, _, cols), delta in zip(parts, deltas):
        ds_ref[b, :, cols] = split(own, p_ref[b, :, cols] * (gp_ref[b, :, cols] - delta))
    for b, heads, kv, cols in parts:
        grad_key = dot(ds_ref[b, :, cols], stacked(q_ref, b, heads), ((1,), (0,))) * SCALE
        dk_ref[b, :, kv] = grad_key[:rows]
        back_ref[b, :, kv] = grad_key[rows:].astype(jnp.bfloat16)
    copy.wait()


def query_kernel(k_ref, hk_ref, ds_ref, dq_ref):
    _, rows, _ = dq_ref.shape
    parts = list(groups(dq_ref))
    keys = [jnp.concatenate([k_ref[b, :, kv], hk_ref[b, :, kv]], axis=0) for b, _, kv, _ in parts]
    products = [dot(ds_ref[b, :, cols], key, ((0,), (0,))) for (b, _, _, cols), key in zip(parts, keys)]
    for (b, heads, _, _), product in zip(parts, products):
        for n, h in enumerate(heads):
            dq_ref[b, :, h * HEAD:(h + 1) * HEAD] = (product[n * rows:(n + 1) * rows] * SCALE).astype(jnp.bfloat16)


def join_kernel(own_ref, back_ref, out_ref):
    out_ref[...] = (own_ref[...] + back_ref[...].astype(jnp.float32)).astype(jnp.bfloat16)


def total_kernel(factor, terms_ref, *refs):
    total_ref = refs[-1]
    total_ref[...] = jnp.sum(terms_ref[...], axis=0, keepdims=True) * factor


def finish_kernel(own_ref, back_ref, total_ref, out_ref, sink_ref):
    join_kernel(own_ref, back_ref, out_ref)
    sink_ref[...] = total_ref[...]


def ring(value, axis, steps):
    count = lax.axis_size(axis)
    return lax.ppermute(value, axis, [(i, (i + steps) % count) for i in range(count)])


def shift(value, axis):
    count = lax.axis_size(axis)
    return lax.ppermute(value, axis, [(i, i + 1) for i in range(count - 1)])


def body(queries, keys, values, dout, sinks):
    batch, rows, width = queries.shape
    kv_width = keys.shape[2]
    dp, ctx = lax.axis_size("dp"), lax.axis_size("ctx")
    assert rows == WINDOW
    bf16, f32 = jnp.bfloat16, jnp.float32
    square = struct((batch, rows, HEADS * rows), f32)
    line = struct((batch, 1, HEADS * rows), f32)
    kv_bf16 = struct((batch, rows, kv_width), bf16)
    product = 2 * batch * HEADS * rows * rows * HEAD

    first = (lax.axis_index("ctx") == 0).astype(jnp.int32).reshape(1)
    halo_keys = ring(keys, "ctx", 1)
    halo_values = shift(values, "ctx")
    q, k, do, score, grad_prob, bias, sink = call(
        load_kernel, "load",
        (struct(queries.shape, bf16), kv_bf16, struct(dout.shape, bf16), square, square,
         struct((1, GROUP * rows), f32), struct((1, HEADS * rows), f32)),
        [SMEM] + [HBM] * 5, (first, sinks, queries, keys, values, dout), 2 * product,
        scratch=[pltpu.VMEM(values.shape, bf16), pltpu.SMEM((HEADS,), f32), pltpu.SemaphoreType.DMA((5,))])
    prob, sink_prob, own_values, back_values = call(
        softmax_kernel, "softmax",
        (pltpu.VMEM(square.shape, f32), pltpu.VMEM(line.shape, f32), pltpu.VMEM(keys.shape, f32),
         pltpu.VMEM(keys.shape, bf16)),
        [VMEM] * 6, (bias, sink, q, do, halo_keys, score), 3 * product)
    back_values = ring(back_values, "ctx", -1)
    terms, dscores, own_keys, back_keys = call(
        grad_kernel, "grad",
        (pltpu.HBM((dp * ctx, HEADS), f32), pltpu.VMEM((batch, 2 * rows, HEADS * rows), bf16), pltpu.VMEM(keys.shape, f32),
         pltpu.VMEM(keys.shape, bf16)),
        [VMEM] * 6, (q, do, halo_values, prob, sink_prob, grad_prob), 3 * product,
        scratch=[pltpu.VMEM(square.shape, f32), pltpu.VMEM((HEADS, rows), f32),
                 pltpu.VMEM((dp * ctx, HEADS), f32), pltpu.SemaphoreType.DMA],
        out_specs=(HBM, VMEM, VMEM, VMEM))
    back_keys = ring(back_keys, "ctx", -1)
    terms = lax.all_to_all(terms, ("dp", "ctx"), 0, 0, tiled=True)
    grad_query, = call(query_kernel, "query", (struct(queries.shape, bf16),), [VMEM] * 3, (k, halo_keys, dscores), 2 * product)
    grad_values, = call(join_kernel, "join", (kv_bf16,), [VMEM] * 2, (own_values, back_values), 0)
    factor = -1.0 / (dp * batch * ctx * rows) ** 0.5
    total, = call(
        functools.partial(total_kernel, factor), "total", (struct((1, HEADS), f32),), [VMEM, HBM, HBM],
        (terms, grad_values, grad_query), 10 ** 10)
    grad_keys, sink_grad = call(
        finish_kernel, "finish", (kv_bf16, struct((1, HEADS), f32)), [VMEM] * 3, (own_keys, back_keys, total), 0)
    return grad_query, grad_keys, grad_values, sink_grad.reshape(HEADS)


def solution(mesh):
    whole = P("dp", "ctx", None)
    return jax.shard_map(
        body,
        mesh=mesh,
        in_specs=(whole, whole, whole, whole, P()),
        out_specs=(whole, whole, whole, P()),
        check_vma=False,
    )
```

```python
import functools
import math

import jax
import jax.numpy as jnp
from jax import lax
from jax.experimental import pallas as pl
from jax.experimental.pallas import tpu as pltpu
from jax.sharding import PartitionSpec as P

HEADS = 16
KV_HEADS = 4
HEAD = 128
WINDOW = 128
GROUP = HEADS // KV_HEADS
SCALE = HEAD ** (-0.5)
LOG2E = 1.4426950408889634
VMEM = pl.BlockSpec(memory_space=pltpu.VMEM)
SMEM = pl.BlockSpec(memory_space=pltpu.SMEM)
HBM = pl.BlockSpec(memory_space=pltpu.HBM)


def dot(a, b, dims):
    return lax.dot_general(a, b, (dims, ((), ())), preferred_element_type=jnp.float32)


def struct(shape, dtype):
    return jax.ShapeDtypeStruct(shape, dtype)


def call(kernel, name, out_shape, in_specs, args, flops, scratch=(), out_specs=None):
    args = [
        pltpu.with_memory_space_constraint(a, pltpu.HBM) if spec is HBM else a
        for a, spec in zip(args, in_specs, strict=True)
    ]
    moved = sum(math.prod(a.shape) * a.dtype.itemsize for a in (*args, *out_shape))
    return pl.pallas_call(
        kernel,
        out_shape=out_shape,
        in_specs=in_specs,
        out_specs=out_specs or (VMEM,) * len(out_shape),
        scratch_shapes=scratch,
        compiler_params=pltpu.CompilerParams(vmem_limit_bytes=32 * 1024 * 1024),
        cost_estimate=pl.CostEstimate(flops=flops, bytes_accessed=moved, transcendentals=0),
        name=name,
    )(*args)


def own_mask(rows, width):
    key_pos = lax.broadcasted_iota(jnp.int32, (rows, width), 0)
    query_pos = lax.rem(lax.broadcasted_iota(jnp.int32, (rows, width), 1), rows)
    return key_pos <= query_pos


def stacked(ref, b, heads):
    return jnp.concatenate([ref[b, :, h * HEAD:(h + 1) * HEAD] for h in heads], axis=0)


def split(own, value):
    value = value.astype(jnp.bfloat16)
    part = value * own.astype(jnp.float32).astype(jnp.bfloat16)
    return jnp.concatenate([part, value - part], axis=0)


def groups(ref):
    batch, rows, _ = ref.shape
    for b in range(batch):
        for g in range(KV_HEADS):
            heads = range(g * GROUP, (g + 1) * GROUP)
            yield b, heads, slice(g * HEAD, (g + 1) * HEAD), slice(g * GROUP * rows, (g + 1) * GROUP * rows)


def load_kernel(first_ref, sinks_in, q_in, k_in, v_in, do_in,
                q_ref, k_ref, do_ref, s_ref, dp_ref, bias_ref, sink_ref, v_ref, sinks_ref, sems):
    _, rows, _ = q_ref.shape
    copies = [
        pltpu.make_async_copy(source, target, sems.at[n])
        for n, (source, target) in enumerate(
            ((k_in, k_ref), (q_in, q_ref), (v_in, v_ref), (do_in, do_ref), (sinks_in, sinks_ref)))
    ]
    for copy in copies:
        copy.start()
    bias_ref[...] = jnp.full(bias_ref.shape, jnp.where(first_ref[0] == 1, -1e30, 0.0), jnp.float32)
    copies[0].wait()
    copies[1].wait()
    for b, heads, kv, cols in groups(q_ref):
        s_ref[b, :, cols] = dot(k_ref[b, :, kv], stacked(q_ref, b, heads), ((1,), (1,)))
    copies[2].wait()
    copies[3].wait()
    for b, heads, kv, cols in groups(q_ref):
        dp_ref[b, :, cols] = dot(v_ref[b, :, kv], stacked(do_ref, b, heads), ((1,), (1,)))
    copies[4].wait()
    for h in range(HEADS):
        sink_ref[:, h * rows:(h + 1) * rows] = jnp.full((1, rows), sinks_ref[h] * LOG2E, jnp.float32)


def fetch_kernel(source, target, sem):
    copy = pltpu.make_async_copy(source, target, sem)
    copy.start()
    copy.wait()


def softmax_kernel(bias_ref, sink_ref, q_ref, do_ref, hk_ref, s_ref, dp_ref,
                   low_ref, back_ref, g_ref, own_ref, p_ref):
    _, rows, _ = q_ref.shape
    own = own_mask(rows, GROUP * rows)
    parts = list(groups(q_ref))
    for b, heads, kv, cols in parts:
        before = dot(hk_ref[b, :, kv], stacked(q_ref, b, heads), ((1,), (1,))) + bias_ref[...]
        p_ref[b, :, cols] = jnp.where(own, s_ref[b, :, cols], before) * (SCALE * LOG2E)
    tops = [jnp.maximum(jnp.max(p_ref[b, :, cols], axis=0, keepdims=True), sink_ref[:, cols])
            for b, _, _, cols in parts]
    sums = []
    for (b, _, _, cols), top in zip(parts, tops):
        weight = jnp.exp2(p_ref[b, :, cols] - top)
        p_ref[b, :, cols] = weight
        sums.append(jnp.sum(weight, axis=0, keepdims=True))
    probs = []
    sink_probs = []
    for (b, _, _, cols), top, total in zip(parts, tops, sums):
        sink_weight = jnp.exp2(sink_ref[:, cols] - top)
        scale = 1.0 / (total + sink_weight)
        sink_probs.append(sink_weight * scale)
        prob = p_ref[b, :, cols] * scale
        p_ref[b, :, cols] = prob
        low_ref[b, :, cols] = prob.astype(jnp.bfloat16)
        probs.append(split(own, prob)[rows:])
    for (b, heads, kv, cols), prob in zip(parts, probs):
        back_ref[b, :, kv] = dot(prob, stacked(do_ref, b, heads), ((1,), (0,))).astype(jnp.bfloat16)
    splits = []
    for (b, _, _, cols), sink_prob in zip(parts, sink_probs):
        prob = p_ref[b, :, cols] * sink_prob
        own_ref[b, :, cols] = jnp.sum(jnp.where(own, prob * dp_ref[b, :, cols], 0.0), axis=0, keepdims=True)
        prob = jnp.where(own, 0.0, prob)
        high = prob.astype(jnp.bfloat16)
        splits.append((high, (prob - high.astype(jnp.float32)).astype(jnp.bfloat16)))
    for (b, heads, _, _), (high, low) in zip(parts, splits):
        for n, h in enumerate(heads):
            part = slice(n * rows, (n + 1) * rows)
            grad = do_ref[b, :, h * HEAD:(h + 1) * HEAD]
            g_ref[b, :, h * HEAD:(h + 1) * HEAD] = dot(
                jnp.concatenate([high[:, part], low[:, part]], axis=1), jnp.concatenate([grad, grad], axis=0),
                ((1,), (0,)))


def terms_kernel(do_ref, hv_ref, g_ref, own_ref, dp_ref, terms_out, gp_ref, sink_ref, terms_ref, sem):
    _, rows, _ = do_ref.shape
    own = own_mask(rows, GROUP * rows)
    parts = list(groups(do_ref))
    for b, heads, kv, _ in parts:
        value = hv_ref[b, :, kv].astype(jnp.float32)
        for h in heads:
            term = jnp.sum(value * g_ref[b, :, h * HEAD:(h + 1) * HEAD], axis=0, keepdims=True)
            term += own_ref[b, :, h * rows:(h + 1) * rows]
            sink_ref[h:h + 1, :] = term if b == 0 else sink_ref[h:h + 1, :] + term
    terms = sink_ref[...]
    high = terms.astype(jnp.bfloat16)
    rest = terms - high.astype(jnp.float32)
    middle = rest.astype(jnp.bfloat16)
    low = (rest - middle.astype(jnp.float32)).astype(jnp.bfloat16)
    split_terms = jnp.concatenate([low, middle, high], axis=1)
    ones = jnp.ones((terms_ref.shape[0], split_terms.shape[1]), jnp.bfloat16)
    terms_ref[...] = dot(ones, split_terms, ((1,), (1,)))
    copy = pltpu.make_async_copy(terms_ref, terms_out, sem)
    copy.start()
    for b, heads, kv, cols in parts:
        before = dot(hv_ref[b, :, kv], stacked(do_ref, b, heads), ((1,), (1,)))
        grad_prob = jnp.where(own, dp_ref[b, :, cols], before)
        gp_ref[b, :, cols] = grad_prob
    copy.wait()


def keys_kernel(q_ref, p_ref, gp_ref, ds_ref, back_ref):
    _, rows, _ = q_ref.shape
    own = own_mask(rows, GROUP * rows)
    parts = list(groups(q_ref))
    deltas = [jnp.sum(p_ref[b, :, cols].astype(jnp.float32) * gp_ref[b, :, cols], axis=0, keepdims=True)
              for b, _, _, cols in parts]
    for (b, _, _, cols), delta in zip(parts, deltas):
        ds_ref[b, :, cols] = split(own, p_ref[b, :, cols].astype(jnp.float32) * (gp_ref[b, :, cols] - delta))
    for b, heads, kv, cols in parts:
        grad_key = dot(ds_ref[b, rows:, cols], stacked(q_ref, b, heads), ((1,), (0,))) * SCALE
        back_ref[b, :, kv] = grad_key.astype(jnp.bfloat16)


def query_kernel(q_ref, k_ref, hk_ref, ds_ref, dq_ref, dk_ref):
    _, rows, _ = dq_ref.shape
    parts = list(groups(dq_ref))
    for b, heads, kv, cols in parts:
        dk_ref[b, :, kv] = dot(ds_ref[b, :rows, cols], stacked(q_ref, b, heads), ((1,), (0,))) * SCALE
    keys = [jnp.concatenate([k_ref[b, :, kv], hk_ref[b, :, kv]], axis=0) for b, _, kv, _ in parts]
    products = [dot(ds_ref[b, :, cols], key, ((0,), (0,))) for (b, _, _, cols), key in zip(parts, keys)]
    for (b, heads, _, _), product in zip(parts, products):
        for n, h in enumerate(heads):
            dq_ref[b, :, h * HEAD:(h + 1) * HEAD] = (product[n * rows:(n + 1) * rows] * SCALE).astype(jnp.bfloat16)


def values_kernel(do_ref, p_ref, back_ref, out_ref):
    _, rows, _ = do_ref.shape
    own = own_mask(rows, GROUP * rows)
    for b, heads, kv, cols in groups(do_ref):
        prob = split(own, p_ref[b, :, cols])[:rows]
        grad_value = dot(prob, stacked(do_ref, b, heads), ((1,), (0,)))
        out_ref[b, :, kv] = (grad_value + back_ref[b, :, kv].astype(jnp.float32)).astype(jnp.bfloat16)


def total_kernel(factor, terms_ref, *refs):
    total_ref = refs[-1]
    total_ref[...] = jnp.sum(terms_ref[...], axis=0, keepdims=True) * factor


def finish_kernel(own_ref, back_ref, total_ref, out_ref, sink_ref):
    out_ref[...] = (own_ref[...] + back_ref[...].astype(jnp.float32)).astype(jnp.bfloat16)
    sink_ref[...] = total_ref[...]


def ring(value, axis, steps):
    count = lax.axis_size(axis)
    return lax.ppermute(value, axis, [(i, (i + steps) % count) for i in range(count)])


def shift(value, axis):
    count = lax.axis_size(axis)
    return lax.ppermute(value, axis, [(i, i + 1) for i in range(count - 1)])


def body(queries, keys, values, dout, sinks):
    batch, rows, width = queries.shape
    kv_width = keys.shape[2]
    dp, ctx = lax.axis_size("dp"), lax.axis_size("ctx")
    assert rows == WINDOW
    bf16, f32 = jnp.bfloat16, jnp.float32
    square = struct((batch, rows, HEADS * rows), f32)
    line = struct((batch, 1, HEADS * rows), f32)
    kv_bf16 = struct((batch, rows, kv_width), bf16)
    product = 2 * batch * HEADS * rows * rows * HEAD

    first = (lax.axis_index("ctx") == 0).astype(jnp.int32).reshape(1)
    halo_keys = ring(keys, "ctx", 1)
    halo_values = shift(values, "ctx")
    q, k, do, score, grad_prob, bias, sink = call(
        load_kernel, "load",
        (struct(queries.shape, bf16), kv_bf16, struct(dout.shape, bf16), square, square,
         struct((1, GROUP * rows), f32), struct((1, HEADS * rows), f32)),
        [SMEM] + [HBM] * 5, (first, sinks, queries, keys, values, dout), 2 * product,
        scratch=[pltpu.VMEM(values.shape, bf16), pltpu.SMEM((HEADS,), f32), pltpu.SemaphoreType.DMA((5,))])
    prob, back_values, halves, own_terms = call(
        softmax_kernel, "softmax",
        (pltpu.VMEM(square.shape, bf16), pltpu.VMEM(keys.shape, bf16),
         pltpu.VMEM(square.shape, f32), pltpu.VMEM(line.shape, f32)),
        [VMEM] * 7, (bias, sink, q, do, halo_keys, score, grad_prob), 4 * product,
        scratch=[pltpu.VMEM(square.shape, f32)])
    back_values = ring(back_values, "ctx", -1)
    terms, grad_prob = call(
        terms_kernel, "terms", (pltpu.HBM((dp * ctx, HEADS), f32), pltpu.VMEM(square.shape, f32)),
        [VMEM] * 5, (do, halo_values, halves, own_terms, grad_prob), product,
        scratch=[pltpu.VMEM((HEADS, rows), f32), pltpu.VMEM((dp * ctx, HEADS), f32), pltpu.SemaphoreType.DMA],
        out_specs=(HBM, VMEM))
    dscores, back_keys = call(
        keys_kernel, "keys",
        (pltpu.VMEM((batch, 2 * rows, HEADS * rows), bf16), pltpu.VMEM(keys.shape, bf16)),
        [VMEM] * 3, (q, prob, grad_prob), 2 * product)
    back_keys = ring(back_keys, "ctx", -1)
    terms = lax.all_to_all(terms, ("dp", "ctx"), 0, 0, tiled=True)
    grad_query, own_keys = call(
        query_kernel, "query", (struct(queries.shape, bf16), pltpu.VMEM(keys.shape, f32)), [VMEM] * 4,
        (q, k, halo_keys, dscores), 3 * product)
    grad_values, = call(values_kernel, "values", (kv_bf16,), [VMEM] * 3, (do, prob, back_values), product)
    factor = -1.0 / (dp * batch * ctx * rows) ** 0.5
    total, = call(
        functools.partial(total_kernel, factor), "total", (struct((1, HEADS), f32),), [VMEM, HBM, HBM],
        (terms, grad_values, grad_query), 10 ** 10)
    grad_keys, sink_grad = call(
        finish_kernel, "finish", (kv_bf16, struct((1, HEADS), f32)), [VMEM] * 3, (own_keys, back_keys, total), 0)
    return grad_query, grad_keys, grad_values, sink_grad.reshape(HEADS)


def solution(mesh):
    whole = P("dp", "ctx", None)
    return jax.shard_map(
        body,
        mesh=mesh,
        in_specs=(whole, whole, whole, whole, P()),
        out_specs=(whole, whole, whole, P()),
        check_vma=False,
    )
```

```python
import functools
import math

import jax
import jax.numpy as jnp
from jax import lax
from jax.experimental import pallas as pl
from jax.experimental.pallas import tpu as pltpu
from jax.sharding import PartitionSpec as P

HEADS = 16
KV_HEADS = 4
HEAD = 128
WINDOW = 128
GROUP = HEADS // KV_HEADS
SCALE = HEAD ** (-0.5)
LOG2E = 1.4426950408889634
VMEM = pl.BlockSpec(memory_space=pltpu.VMEM)
SMEM = pl.BlockSpec(memory_space=pltpu.SMEM)
HBM = pl.BlockSpec(memory_space=pltpu.HBM)


def dot(a, b, dims):
    return lax.dot_general(a, b, (dims, ((), ())), preferred_element_type=jnp.float32)


def struct(shape, dtype):
    return jax.ShapeDtypeStruct(shape, dtype)


def call(kernel, name, out_shape, in_specs, args, flops, scratch=(), out_specs=None):
    args = [
        pltpu.with_memory_space_constraint(a, pltpu.HBM) if spec is HBM else a
        for a, spec in zip(args, in_specs, strict=True)
    ]
    moved = sum(math.prod(a.shape) * a.dtype.itemsize for a in (*args, *out_shape))
    return pl.pallas_call(
        kernel,
        out_shape=out_shape,
        in_specs=in_specs,
        out_specs=out_specs or (VMEM,) * len(out_shape),
        scratch_shapes=scratch,
        compiler_params=pltpu.CompilerParams(vmem_limit_bytes=32 * 1024 * 1024),
        cost_estimate=pl.CostEstimate(flops=flops, bytes_accessed=moved, transcendentals=0),
        name=name,
    )(*args)


def own_mask(rows, width):
    key_pos = lax.broadcasted_iota(jnp.int32, (rows, width), 0)
    query_pos = lax.rem(lax.broadcasted_iota(jnp.int32, (rows, width), 1), rows)
    return key_pos <= query_pos


def stacked(ref, b, heads):
    return jnp.concatenate([ref[b, :, h * HEAD:(h + 1) * HEAD] for h in heads], axis=0)


def split(own, value):
    value = value.astype(jnp.bfloat16)
    part = value * own.astype(jnp.float32).astype(jnp.bfloat16)
    return jnp.concatenate([part, value - part], axis=0)


def groups(ref):
    batch, rows, _ = ref.shape
    for b in range(batch):
        for g in range(KV_HEADS):
            heads = range(g * GROUP, (g + 1) * GROUP)
            yield b, heads, slice(g * HEAD, (g + 1) * HEAD), slice(g * GROUP * rows, (g + 1) * GROUP * rows)


def load_kernel(first_ref, sinks_in, q_in, k_in, v_in, do_in,
                q_ref, k_ref, do_ref, s_ref, dp_ref, bias_ref, sink_ref, v_ref, sinks_ref, sems):
    _, rows, _ = q_ref.shape
    copies = [
        pltpu.make_async_copy(source, target, sems.at[n])
        for n, (source, target) in enumerate(
            ((k_in, k_ref), (q_in, q_ref), (v_in, v_ref), (do_in, do_ref), (sinks_in, sinks_ref)))
    ]
    for copy in copies:
        copy.start()
    bias_ref[...] = jnp.full(bias_ref.shape, jnp.where(first_ref[0] == 1, -1e30, 0.0), jnp.float32)
    copies[0].wait()
    copies[1].wait()
    for b, heads, kv, cols in groups(q_ref):
        s_ref[b, :, cols] = dot(k_ref[b, :, kv], stacked(q_ref, b, heads), ((1,), (1,)))
    copies[2].wait()
    copies[3].wait()
    for b, heads, kv, cols in groups(q_ref):
        dp_ref[b, :, cols] = dot(v_ref[b, :, kv], stacked(do_ref, b, heads), ((1,), (1,)))
    copies[4].wait()
    for h in range(HEADS):
        sink_ref[:, h * rows:(h + 1) * rows] = jnp.full((1, rows), sinks_ref[h] * LOG2E, jnp.float32)


def fetch_kernel(source, target, sem):
    copy = pltpu.make_async_copy(source, target, sem)
    copy.start()
    copy.wait()


def softmax_kernel(bias_ref, sink_ref, q_ref, do_ref, hk_ref, s_ref, dp_ref,
                   low_ref, back_ref, g_ref, own_ref, p_ref):
    _, rows, _ = q_ref.shape
    own = own_mask(rows, GROUP * rows)
    parts = list(groups(q_ref))
    for b, heads, kv, cols in parts:
        before = dot(hk_ref[b, :, kv], stacked(q_ref, b, heads), ((1,), (1,))) + bias_ref[...]
        p_ref[b, :, cols] = jnp.where(own, s_ref[b, :, cols], before) * (SCALE * LOG2E)
    tops = [jnp.maximum(jnp.max(p_ref[b, :, cols], axis=0, keepdims=True), sink_ref[:, cols])
            for b, _, _, cols in parts]
    sums = []
    for (b, _, _, cols), top in zip(parts, tops):
        weight = jnp.exp2(p_ref[b, :, cols] - top)
        p_ref[b, :, cols] = weight
        sums.append(jnp.sum(weight, axis=0, keepdims=True))
    probs = []
    sink_probs = []
    for (b, _, _, cols), top, total in zip(parts, tops, sums):
        sink_weight = jnp.exp2(sink_ref[:, cols] - top)
        scale = 1.0 / (total + sink_weight)
        sink_probs.append(sink_weight * scale)
        prob = p_ref[b, :, cols] * scale
        p_ref[b, :, cols] = prob
        low_ref[b, :, cols] = prob.astype(jnp.bfloat16)
        probs.append(split(own, prob)[rows:])
    for (b, heads, kv, cols), prob in zip(parts, probs):
        back_ref[b, :, kv] = dot(prob, stacked(do_ref, b, heads), ((1,), (0,))).astype(jnp.bfloat16)
    splits = []
    for (b, _, _, cols), sink_prob in zip(parts, sink_probs):
        prob = p_ref[b, :, cols] * sink_prob
        own_ref[b, :, cols] = jnp.sum(jnp.where(own, prob * dp_ref[b, :, cols], 0.0), axis=0, keepdims=True)
        prob = jnp.where(own, 0.0, prob)
        high = prob.astype(jnp.bfloat16)
        splits.append((high, (prob - high.astype(jnp.float32)).astype(jnp.bfloat16)))
    for (b, heads, _, _), (high, low) in zip(parts, splits):
        for n, h in enumerate(heads):
            part = slice(n * rows, (n + 1) * rows)
            grad = do_ref[b, :, h * HEAD:(h + 1) * HEAD]
            g_ref[b, :, h * HEAD:(h + 1) * HEAD] = dot(
                jnp.concatenate([high[:, part], low[:, part]], axis=1), jnp.concatenate([grad, grad], axis=0),
                ((1,), (0,)))


def terms_kernel(do_ref, hv_ref, g_ref, own_ref, p_ref, dp_ref, terms_out, gp_ref, sink_ref, terms_ref, sem):
    _, rows, _ = do_ref.shape
    own = own_mask(rows, GROUP * rows)
    parts = list(groups(do_ref))
    for b, heads, kv, _ in parts:
        value = hv_ref[b, :, kv].astype(jnp.float32)
        for h in heads:
            term = jnp.sum(value * g_ref[b, :, h * HEAD:(h + 1) * HEAD], axis=0, keepdims=True)
            term += own_ref[b, :, h * rows:(h + 1) * rows]
            sink_ref[h:h + 1, :] = term if b == 0 else sink_ref[h:h + 1, :] + term
    terms = sink_ref[...]
    high = terms.astype(jnp.bfloat16)
    rest = terms - high.astype(jnp.float32)
    middle = rest.astype(jnp.bfloat16)
    low = (rest - middle.astype(jnp.float32)).astype(jnp.bfloat16)
    split_terms = jnp.concatenate([low, middle, high], axis=1)
    ones = jnp.ones((terms_ref.shape[0], split_terms.shape[1]), jnp.bfloat16)
    terms_ref[...] = dot(ones, split_terms, ((1,), (1,)))
    copy = pltpu.make_async_copy(terms_ref, terms_out, sem)
    copy.start()
    for b, heads, kv, cols in parts:
        before = dot(hv_ref[b, :, kv], stacked(do_ref, b, heads), ((1,), (1,)))
        grad_prob = jnp.where(own, dp_ref[b, :, cols], before)
        gp_ref[b, :rows, cols] = grad_prob
        gp_ref[b, rows:rows + 1, cols] = jnp.sum(
            p_ref[b, :, cols].astype(jnp.float32) * grad_prob, axis=0, keepdims=True)
    copy.wait()


def keys_kernel(q_ref, p_ref, gp_ref, ds_ref, back_ref):
    _, rows, _ = q_ref.shape
    own = own_mask(rows, GROUP * rows)
    parts = list(groups(q_ref))
    dscores = []
    for b, _, _, cols in parts:
        delta = gp_ref[b, rows:rows + 1, cols]
        dscores.append((p_ref[b, :, cols].astype(jnp.float32) * (gp_ref[b, :rows, cols] - delta)).astype(jnp.bfloat16))
        ds_ref[b, :, cols] = dscores[-1]
    for (b, heads, kv, cols), dscore in zip(parts, dscores):
        grad_key = dot(split(own, dscore)[rows:], stacked(q_ref, b, heads), ((1,), (0,))) * SCALE
        back_ref[b, :, kv] = grad_key.astype(jnp.bfloat16)


def query_kernel(q_ref, k_ref, hk_ref, ds_ref, dq_ref, dk_ref):
    _, rows, _ = dq_ref.shape
    own = own_mask(rows, GROUP * rows)
    parts = list(groups(dq_ref))
    dscores = [split(own, ds_ref[b, :, cols]) for b, _, _, cols in parts]
    for (b, heads, kv, _), dscore in zip(parts, dscores):
        dk_ref[b, :, kv] = dot(dscore[:rows], stacked(q_ref, b, heads), ((1,), (0,))) * SCALE
    keys = [jnp.concatenate([k_ref[b, :, kv], hk_ref[b, :, kv]], axis=0) for b, _, kv, _ in parts]
    products = [dot(dscore, key, ((0,), (0,))) for dscore, key in zip(dscores, keys)]
    for (b, heads, _, _), product in zip(parts, products):
        for n, h in enumerate(heads):
            dq_ref[b, :, h * HEAD:(h + 1) * HEAD] = (product[n * rows:(n + 1) * rows] * SCALE).astype(jnp.bfloat16)


def values_kernel(do_ref, p_ref, back_ref, out_ref):
    _, rows, _ = do_ref.shape
    own = own_mask(rows, GROUP * rows)
    for b, heads, kv, cols in groups(do_ref):
        prob = split(own, p_ref[b, :, cols])[:rows]
        grad_value = dot(prob, stacked(do_ref, b, heads), ((1,), (0,)))
        out_ref[b, :, kv] = (grad_value + back_ref[b, :, kv].astype(jnp.float32)).astype(jnp.bfloat16)


def total_kernel(factor, terms_ref, *refs):
    total_ref = refs[-1]
    total_ref[...] = jnp.sum(terms_ref[...], axis=0, keepdims=True) * factor


def finish_kernel(own_ref, back_ref, total_ref, out_ref, sink_ref):
    out_ref[...] = (own_ref[...] + back_ref[...].astype(jnp.float32)).astype(jnp.bfloat16)
    sink_ref[...] = total_ref[...]


def ring(value, axis, steps):
    count = lax.axis_size(axis)
    return lax.ppermute(value, axis, [(i, (i + steps) % count) for i in range(count)])


def shift(value, axis):
    count = lax.axis_size(axis)
    return lax.ppermute(value, axis, [(i, i + 1) for i in range(count - 1)])


def body(queries, keys, values, dout, sinks):
    batch, rows, width = queries.shape
    kv_width = keys.shape[2]
    dp, ctx = lax.axis_size("dp"), lax.axis_size("ctx")
    assert rows == WINDOW
    bf16, f32 = jnp.bfloat16, jnp.float32
    square = struct((batch, rows, HEADS * rows), f32)
    line = struct((batch, 1, HEADS * rows), f32)
    kv_bf16 = struct((batch, rows, kv_width), bf16)
    product = 2 * batch * HEADS * rows * rows * HEAD

    first = (lax.axis_index("ctx") == 0).astype(jnp.int32).reshape(1)
    halo_keys = ring(keys, "ctx", 1)
    halo_values = shift(values, "ctx")
    q, k, do, score, grad_prob, bias, sink = call(
        load_kernel, "load",
        (struct(queries.shape, bf16), kv_bf16, struct(dout.shape, bf16), square, square,
         struct((1, GROUP * rows), f32), struct((1, HEADS * rows), f32)),
        [SMEM] + [HBM] * 5, (first, sinks, queries, keys, values, dout), 2 * product,
        scratch=[pltpu.VMEM(values.shape, bf16), pltpu.SMEM((HEADS,), f32), pltpu.SemaphoreType.DMA((5,))])
    prob, back_values, halves, own_terms = call(
        softmax_kernel, "softmax",
        (pltpu.VMEM(square.shape, bf16), pltpu.VMEM(keys.shape, bf16),
         pltpu.VMEM(square.shape, f32), pltpu.VMEM(line.shape, f32)),
        [VMEM] * 7, (bias, sink, q, do, halo_keys, score, grad_prob), 4 * product,
        scratch=[pltpu.VMEM(square.shape, f32)])
    back_values = ring(back_values, "ctx", -1)
    terms, grad_prob = call(
        terms_kernel, "terms", (pltpu.HBM((dp * ctx, HEADS), f32), pltpu.VMEM((batch, rows + 8, HEADS * rows), f32)),
        [VMEM] * 6, (do, halo_values, halves, own_terms, prob, grad_prob), product,
        scratch=[pltpu.VMEM((HEADS, rows), f32), pltpu.VMEM((dp * ctx, HEADS), f32), pltpu.SemaphoreType.DMA],
        out_specs=(HBM, VMEM))
    dscores, back_keys = call(
        keys_kernel, "keys",
        (pltpu.VMEM(square.shape, bf16), pltpu.VMEM(keys.shape, bf16)),
        [VMEM] * 3, (q, prob, grad_prob), 2 * product)
    back_keys = ring(back_keys, "ctx", -1)
    terms = lax.all_to_all(terms, ("dp", "ctx"), 0, 0, tiled=True)
    grad_query, own_keys = call(
        query_kernel, "query", (struct(queries.shape, bf16), pltpu.VMEM(keys.shape, f32)), [VMEM] * 4,
        (q, k, halo_keys, dscores), 3 * product)
    grad_values, = call(values_kernel, "values", (kv_bf16,), [VMEM] * 3, (do, prob, back_values), product)
    factor = -1.0 / (dp * batch * ctx * rows) ** 0.5
    total, = call(
        functools.partial(total_kernel, factor), "total", (struct((1, HEADS), f32),), [VMEM, HBM, HBM],
        (terms, grad_values, grad_query), 10 ** 10)
    grad_keys, sink_grad = call(
        finish_kernel, "finish", (kv_bf16, struct((1, HEADS), f32)), [VMEM] * 3, (own_keys, back_keys, total), 0)
    return grad_query, grad_keys, grad_values, sink_grad.reshape(HEADS)


def solution(mesh):
    whole = P("dp", "ctx", None)
    return jax.shard_map(
        body,
        mesh=mesh,
        in_specs=(whole, whole, whole, whole, P()),
        out_specs=(whole, whole, whole, P()),
        check_vma=False,
    )
```

```python
import functools
import math

import jax
import jax.numpy as jnp
from jax import lax
from jax.experimental import pallas as pl
from jax.experimental.pallas import tpu as pltpu
from jax.sharding import PartitionSpec as P

HEADS = 16
KV_HEADS = 4
HEAD = 128
WINDOW = 128
GROUP = HEADS // KV_HEADS
SCALE = HEAD ** (-0.5)
LOG2E = 1.4426950408889634
VMEM = pl.BlockSpec(memory_space=pltpu.VMEM)
SMEM = pl.BlockSpec(memory_space=pltpu.SMEM)
HBM = pl.BlockSpec(memory_space=pltpu.HBM)


def dot(a, b, dims):
    return lax.dot_general(a, b, (dims, ((), ())), preferred_element_type=jnp.float32)


def struct(shape, dtype):
    return jax.ShapeDtypeStruct(shape, dtype)


def call(kernel, name, out_shape, in_specs, args, flops, scratch=(), out_specs=None):
    args = [
        pltpu.with_memory_space_constraint(a, pltpu.HBM) if spec is HBM else a
        for a, spec in zip(args, in_specs, strict=True)
    ]
    moved = sum(math.prod(a.shape) * a.dtype.itemsize for a in (*args, *out_shape))
    return pl.pallas_call(
        kernel,
        out_shape=out_shape,
        in_specs=in_specs,
        out_specs=out_specs or (VMEM,) * len(out_shape),
        scratch_shapes=scratch,
        compiler_params=pltpu.CompilerParams(vmem_limit_bytes=32 * 1024 * 1024),
        cost_estimate=pl.CostEstimate(flops=flops, bytes_accessed=moved, transcendentals=0),
        name=name,
    )(*args)


def own_mask(rows, width):
    key_pos = lax.broadcasted_iota(jnp.int32, (rows, width), 0)
    query_pos = lax.rem(lax.broadcasted_iota(jnp.int32, (rows, width), 1), rows)
    return key_pos <= query_pos


def stacked(ref, b, heads):
    return jnp.concatenate([ref[b, :, h * HEAD:(h + 1) * HEAD] for h in heads], axis=0)


def split(own, value):
    value = value.astype(jnp.bfloat16)
    part = value * own.astype(jnp.float32).astype(jnp.bfloat16)
    return jnp.concatenate([part, value - part], axis=0)


def groups(ref):
    batch, rows, _ = ref.shape
    for b in range(batch):
        for g in range(KV_HEADS):
            heads = range(g * GROUP, (g + 1) * GROUP)
            yield b, heads, slice(g * HEAD, (g + 1) * HEAD), slice(g * GROUP * rows, (g + 1) * GROUP * rows)


def load_kernel(first_ref, sinks_in, q_in, k_in, v_in, do_in,
                q_ref, k_ref, do_ref, s_ref, dp_ref, bias_ref, sink_ref, v_ref, sinks_ref, sems):
    _, rows, _ = q_ref.shape
    copies = [
        pltpu.make_async_copy(source, target, sems.at[n])
        for n, (source, target) in enumerate(
            ((k_in, k_ref), (q_in, q_ref), (v_in, v_ref), (do_in, do_ref), (sinks_in, sinks_ref)))
    ]
    for copy in copies:
        copy.start()
    bias_ref[...] = jnp.full(bias_ref.shape, jnp.where(first_ref[0] == 1, -1e30, 0.0), jnp.float32)
    copies[0].wait()
    copies[1].wait()
    for b, heads, kv, cols in groups(q_ref):
        s_ref[b, :, cols] = dot(k_ref[b, :, kv], stacked(q_ref, b, heads), ((1,), (1,)))
    copies[2].wait()
    copies[3].wait()
    for b, heads, kv, cols in groups(q_ref):
        dp_ref[b, :, cols] = dot(v_ref[b, :, kv], stacked(do_ref, b, heads), ((1,), (1,)))
    copies[4].wait()
    for h in range(HEADS):
        sink_ref[:, h * rows:(h + 1) * rows] = jnp.full((1, rows), sinks_ref[h] * LOG2E, jnp.float32)


def fetch_kernel(source, target, sem):
    copy = pltpu.make_async_copy(source, target, sem)
    copy.start()
    copy.wait()


def softmax_kernel(bias_ref, sink_ref, q_ref, do_ref, hk_ref, s_ref, dp_ref,
                   low_ref, back_ref, g_ref, own_ref, p_ref):
    _, rows, _ = q_ref.shape
    own = own_mask(rows, GROUP * rows)
    parts = list(groups(q_ref))
    for b, heads, kv, cols in parts:
        before = dot(hk_ref[b, :, kv], stacked(q_ref, b, heads), ((1,), (1,))) + bias_ref[...]
        p_ref[b, :, cols] = jnp.where(own, s_ref[b, :, cols], before) * (SCALE * LOG2E)
    tops = [jnp.maximum(jnp.max(p_ref[b, :, cols], axis=0, keepdims=True), sink_ref[:, cols])
            for b, _, _, cols in parts]
    sums = []
    for (b, _, _, cols), top in zip(parts, tops):
        weight = jnp.exp2(p_ref[b, :, cols] - top)
        p_ref[b, :, cols] = weight
        sums.append(jnp.sum(weight, axis=0, keepdims=True))
    probs = []
    sink_probs = []
    for (b, _, _, cols), top, total in zip(parts, tops, sums):
        sink_weight = jnp.exp2(sink_ref[:, cols] - top)
        scale = 1.0 / (total + sink_weight)
        sink_probs.append(sink_weight * scale)
        prob = p_ref[b, :, cols] * scale
        p_ref[b, :, cols] = prob
        low_ref[b, :, cols] = prob.astype(jnp.bfloat16)
        probs.append(split(own, prob)[rows:])
    for (b, heads, kv, cols), prob in zip(parts, probs):
        back_ref[b, :, kv] = dot(prob, stacked(do_ref, b, heads), ((1,), (0,))).astype(jnp.bfloat16)
    splits = []
    for (b, _, _, cols), sink_prob in zip(parts, sink_probs):
        prob = p_ref[b, :, cols] * sink_prob
        own_ref[b, :, cols] = jnp.sum(jnp.where(own, prob * dp_ref[b, :, cols], 0.0), axis=0, keepdims=True)
        splits.append(split(own, prob)[rows:])
    for (b, heads, _, _), high in zip(parts, splits):
        for n, h in enumerate(heads):
            part = slice(n * rows, (n + 1) * rows)
            grad = do_ref[b, :, h * HEAD:(h + 1) * HEAD]
            g_ref[b, :, h * HEAD:(h + 1) * HEAD] = dot(high[:, part], grad, ((1,), (0,)))


def terms_kernel(do_ref, hv_ref, g_ref, own_ref, p_ref, dp_ref, terms_out, gp_ref, sink_ref, terms_ref, sem):
    _, rows, _ = do_ref.shape
    own = own_mask(rows, GROUP * rows)
    parts = list(groups(do_ref))
    for b, heads, kv, _ in parts:
        value = hv_ref[b, :, kv].astype(jnp.float32)
        for h in heads:
            term = jnp.sum(value * g_ref[b, :, h * HEAD:(h + 1) * HEAD], axis=0, keepdims=True)
            term += own_ref[b, :, h * rows:(h + 1) * rows]
            sink_ref[h:h + 1, :] = term if b == 0 else sink_ref[h:h + 1, :] + term
    terms = sink_ref[...]
    high = terms.astype(jnp.bfloat16)
    rest = terms - high.astype(jnp.float32)
    middle = rest.astype(jnp.bfloat16)
    low = (rest - middle.astype(jnp.float32)).astype(jnp.bfloat16)
    split_terms = jnp.concatenate([low, middle, high], axis=1)
    ones = jnp.ones((terms_ref.shape[0], split_terms.shape[1]), jnp.bfloat16)
    terms_ref[...] = dot(ones, split_terms, ((1,), (1,)))
    copy = pltpu.make_async_copy(terms_ref, terms_out, sem)
    copy.start()
    for b, heads, kv, cols in parts:
        before = dot(hv_ref[b, :, kv], stacked(do_ref, b, heads), ((1,), (1,)))
        grad_prob = jnp.where(own, dp_ref[b, :, cols], before)
        gp_ref[b, :rows, cols] = grad_prob
        gp_ref[b, rows:rows + 1, cols] = jnp.sum(
            p_ref[b, :, cols].astype(jnp.float32) * grad_prob, axis=0, keepdims=True)
    copy.wait()


def keys_kernel(q_ref, p_ref, gp_ref, ds_ref, back_ref):
    _, rows, _ = q_ref.shape
    own = own_mask(rows, GROUP * rows)
    parts = list(groups(q_ref))
    dscores = []
    for b, _, _, cols in parts:
        delta = gp_ref[b, rows:rows + 1, cols]
        dscores.append((p_ref[b, :, cols].astype(jnp.float32) * (gp_ref[b, :rows, cols] - delta)).astype(jnp.bfloat16))
        ds_ref[b, :, cols] = dscores[-1]
    for (b, heads, kv, cols), dscore in zip(parts, dscores):
        grad_key = dot(split(own, dscore)[rows:], stacked(q_ref, b, heads), ((1,), (0,))) * SCALE
        back_ref[b, :, kv] = grad_key.astype(jnp.bfloat16)


def query_kernel(q_ref, k_ref, hk_ref, ds_ref, dq_ref, dk_ref):
    _, rows, _ = dq_ref.shape
    own = own_mask(rows, GROUP * rows)
    parts = list(groups(dq_ref))
    dscores = [split(own, ds_ref[b, :, cols]) for b, _, _, cols in parts]
    for (b, heads, kv, _), dscore in zip(parts, dscores):
        dk_ref[b, :, kv] = dot(dscore[:rows], stacked(q_ref, b, heads), ((1,), (0,))) * SCALE
    keys = [jnp.concatenate([k_ref[b, :, kv], hk_ref[b, :, kv]], axis=0) for b, _, kv, _ in parts]
    products = [dot(dscore, key, ((0,), (0,))) for dscore, key in zip(dscores, keys)]
    for (b, heads, _, _), product in zip(parts, products):
        for n, h in enumerate(heads):
            dq_ref[b, :, h * HEAD:(h + 1) * HEAD] = (product[n * rows:(n + 1) * rows] * SCALE).astype(jnp.bfloat16)


def values_kernel(do_ref, p_ref, back_ref, out_ref):
    _, rows, _ = do_ref.shape
    own = own_mask(rows, GROUP * rows)
    for b, heads, kv, cols in groups(do_ref):
        prob = split(own, p_ref[b, :, cols])[:rows]
        grad_value = dot(prob, stacked(do_ref, b, heads), ((1,), (0,)))
        out_ref[b, :, kv] = (grad_value + back_ref[b, :, kv].astype(jnp.float32)).astype(jnp.bfloat16)


def total_kernel(factor, terms_ref, *refs):
    total_ref = refs[-1]
    total_ref[...] = jnp.sum(terms_ref[...], axis=0, keepdims=True) * factor


def finish_kernel(own_ref, back_ref, total_ref, out_ref, sink_ref):
    out_ref[...] = (own_ref[...] + back_ref[...].astype(jnp.float32)).astype(jnp.bfloat16)
    sink_ref[...] = total_ref[...]


def ring(value, axis, steps):
    count = lax.axis_size(axis)
    return lax.ppermute(value, axis, [(i, (i + steps) % count) for i in range(count)])


def shift(value, axis):
    count = lax.axis_size(axis)
    return lax.ppermute(value, axis, [(i, i + 1) for i in range(count - 1)])


def body(queries, keys, values, dout, sinks):
    batch, rows, width = queries.shape
    kv_width = keys.shape[2]
    dp, ctx = lax.axis_size("dp"), lax.axis_size("ctx")
    assert rows == WINDOW
    bf16, f32 = jnp.bfloat16, jnp.float32
    square = struct((batch, rows, HEADS * rows), f32)
    line = struct((batch, 1, HEADS * rows), f32)
    kv_bf16 = struct((batch, rows, kv_width), bf16)
    product = 2 * batch * HEADS * rows * rows * HEAD

    first = (lax.axis_index("ctx") == 0).astype(jnp.int32).reshape(1)
    halo_keys = ring(keys, "ctx", 1)
    halo_values = shift(values, "ctx")
    q, k, do, score, grad_prob, bias, sink = call(
        load_kernel, "load",
        (struct(queries.shape, bf16), kv_bf16, struct(dout.shape, bf16), square, square,
         struct((1, GROUP * rows), f32), struct((1, HEADS * rows), f32)),
        [SMEM] + [HBM] * 5, (first, sinks, queries, keys, values, dout), 2 * product,
        scratch=[pltpu.VMEM(values.shape, bf16), pltpu.SMEM((HEADS,), f32), pltpu.SemaphoreType.DMA((5,))])
    prob, back_values, halves, own_terms = call(
        softmax_kernel, "softmax",
        (pltpu.VMEM(square.shape, bf16), pltpu.VMEM(keys.shape, bf16),
         pltpu.VMEM(square.shape, f32), pltpu.VMEM(line.shape, f32)),
        [VMEM] * 7, (bias, sink, q, do, halo_keys, score, grad_prob), 4 * product,
        scratch=[pltpu.VMEM(square.shape, f32)])
    back_values = ring(back_values, "ctx", -1)
    terms, grad_prob = call(
        terms_kernel, "terms", (pltpu.HBM((dp * ctx, HEADS), f32), pltpu.VMEM((batch, rows + 8, HEADS * rows), f32)),
        [VMEM] * 6, (do, halo_values, halves, own_terms, prob, grad_prob), product,
        scratch=[pltpu.VMEM((HEADS, rows), f32), pltpu.VMEM((dp * ctx, HEADS), f32), pltpu.SemaphoreType.DMA],
        out_specs=(HBM, VMEM))
    dscores, back_keys = call(
        keys_kernel, "keys",
        (pltpu.VMEM(square.shape, bf16), pltpu.VMEM(keys.shape, bf16)),
        [VMEM] * 3, (q, prob, grad_prob), 2 * product)
    back_keys = ring(back_keys, "ctx", -1)
    terms = lax.all_to_all(terms, ("dp", "ctx"), 0, 0, tiled=True)
    grad_query, own_keys = call(
        query_kernel, "query", (struct(queries.shape, bf16), pltpu.VMEM(keys.shape, f32)), [VMEM] * 4,
        (q, k, halo_keys, dscores), 3 * product)
    grad_values, = call(values_kernel, "values", (kv_bf16,), [VMEM] * 3, (do, prob, back_values), product)
    factor = -1.0 / (dp * batch * ctx * rows) ** 0.5
    total, = call(
        functools.partial(total_kernel, factor), "total", (struct((1, HEADS), f32),), [VMEM, HBM, HBM],
        (terms, grad_values, grad_query), 10 ** 10)
    grad_keys, sink_grad = call(
        finish_kernel, "finish", (kv_bf16, struct((1, HEADS), f32)), [VMEM] * 3, (own_keys, back_keys, total), 0)
    return grad_query, grad_keys, grad_values, sink_grad.reshape(HEADS)


def solution(mesh):
    whole = P("dp", "ctx", None)
    return jax.shard_map(
        body,
        mesh=mesh,
        in_specs=(whole, whole, whole, whole, P()),
        out_specs=(whole, whole, whole, P()),
        check_vma=False,
    )
```

```python
import functools
import math

import jax
import jax.numpy as jnp
from jax import lax
from jax.experimental import pallas as pl
from jax.experimental.pallas import tpu as pltpu
from jax.sharding import PartitionSpec as P

HEADS = 16
KV_HEADS = 4
HEAD = 128
WINDOW = 128
GROUP = HEADS // KV_HEADS
SCALE = HEAD ** (-0.5)
LOG2E = 1.4426950408889634
VMEM = pl.BlockSpec(memory_space=pltpu.VMEM)
SMEM = pl.BlockSpec(memory_space=pltpu.SMEM)
HBM = pl.BlockSpec(memory_space=pltpu.HBM)


def dot(a, b, dims):
    return lax.dot_general(a, b, (dims, ((), ())), preferred_element_type=jnp.float32)


def struct(shape, dtype):
    return jax.ShapeDtypeStruct(shape, dtype)


def call(kernel, name, out_shape, in_specs, args, flops, scratch=(), out_specs=None):
    args = [
        pltpu.with_memory_space_constraint(a, pltpu.HBM) if spec is HBM else a
        for a, spec in zip(args, in_specs, strict=True)
    ]
    moved = sum(math.prod(a.shape) * a.dtype.itemsize for a in (*args, *out_shape))
    return pl.pallas_call(
        kernel,
        out_shape=out_shape,
        in_specs=in_specs,
        out_specs=out_specs or (VMEM,) * len(out_shape),
        scratch_shapes=scratch,
        compiler_params=pltpu.CompilerParams(vmem_limit_bytes=32 * 1024 * 1024),
        cost_estimate=pl.CostEstimate(flops=flops, bytes_accessed=moved, transcendentals=0),
        name=name,
    )(*args)


def own_mask(rows, width):
    key_pos = lax.broadcasted_iota(jnp.int32, (rows, width), 0)
    query_pos = lax.rem(lax.broadcasted_iota(jnp.int32, (rows, width), 1), rows)
    return key_pos <= query_pos


def stacked(ref, b, heads):
    return jnp.concatenate([ref[b, :, h * HEAD:(h + 1) * HEAD] for h in heads], axis=0)


def split(own, value):
    value = value.astype(jnp.bfloat16)
    part = value * own.astype(jnp.float32).astype(jnp.bfloat16)
    return jnp.concatenate([part, value - part], axis=0)


def groups(ref):
    batch, rows, _ = ref.shape
    for b in range(batch):
        for g in range(KV_HEADS):
            heads = range(g * GROUP, (g + 1) * GROUP)
            yield b, heads, slice(g * HEAD, (g + 1) * HEAD), slice(g * GROUP * rows, (g + 1) * GROUP * rows)


def load_kernel(first_ref, sinks_in, q_in, k_in, v_in, do_in,
                q_ref, k_ref, do_ref, s_ref, dp_ref, bias_ref, sink_ref, v_ref, sinks_ref, sems):
    _, rows, _ = q_ref.shape
    copies = [
        pltpu.make_async_copy(source, target, sems.at[n])
        for n, (source, target) in enumerate(
            ((k_in, k_ref), (q_in, q_ref), (v_in, v_ref), (do_in, do_ref), (sinks_in, sinks_ref)))
    ]
    for copy in copies:
        copy.start()
    bias_ref[...] = jnp.full(bias_ref.shape, jnp.where(first_ref[0] == 1, -1e30, 0.0), jnp.float32)
    copies[0].wait()
    copies[1].wait()
    for b, heads, kv, cols in groups(q_ref):
        s_ref[b, :, cols] = dot(k_ref[b, :, kv], stacked(q_ref, b, heads), ((1,), (1,)))
    copies[2].wait()
    copies[3].wait()
    for b, heads, kv, cols in groups(q_ref):
        dp_ref[b, :, cols] = dot(v_ref[b, :, kv], stacked(do_ref, b, heads), ((1,), (1,)))
    copies[4].wait()
    for h in range(HEADS):
        sink_ref[:, h * rows:(h + 1) * rows] = jnp.full((1, rows), sinks_ref[h] * LOG2E, jnp.float32)


def fetch_kernel(source, target, sem):
    copy = pltpu.make_async_copy(source, target, sem)
    copy.start()
    copy.wait()


def softmax_kernel(bias_ref, sink_ref, q_ref, do_ref, hk_ref, s_ref, dp_ref,
                   low_ref, back_ref, g_ref, own_ref, p_ref):
    _, rows, _ = q_ref.shape
    own = own_mask(rows, GROUP * rows)
    parts = list(groups(q_ref))
    for b, heads, kv, cols in parts:
        before = dot(hk_ref[b, :, kv], stacked(q_ref, b, heads), ((1,), (1,))) + bias_ref[...]
        p_ref[b, :, cols] = jnp.where(own, s_ref[b, :, cols], before) * (SCALE * LOG2E)
    tops = [jnp.maximum(jnp.max(p_ref[b, :, cols], axis=0, keepdims=True), sink_ref[:, cols])
            for b, _, _, cols in parts]
    sums = []
    for (b, _, _, cols), top in zip(parts, tops):
        weight = jnp.exp2(p_ref[b, :, cols] - top)
        p_ref[b, :, cols] = weight
        sums.append(jnp.sum(weight, axis=0, keepdims=True))
    probs = []
    sink_probs = []
    for (b, _, _, cols), top, total in zip(parts, tops, sums):
        sink_weight = jnp.exp2(sink_ref[:, cols] - top)
        scale = 1.0 / (total + sink_weight)
        sink_probs.append(sink_weight * scale)
        prob = p_ref[b, :, cols] * scale
        p_ref[b, :, cols] = prob
        low_ref[b, :, cols] = prob.astype(jnp.bfloat16)
        probs.append(split(own, prob)[rows:])
    for (b, heads, kv, cols), prob in zip(parts, probs):
        back_ref[b, :, kv] = dot(prob, stacked(do_ref, b, heads), ((1,), (0,))).astype(jnp.bfloat16)
    splits = []
    for (b, _, _, cols), sink_prob in zip(parts, sink_probs):
        prob = p_ref[b, :, cols] * sink_prob
        own_ref[b, :, cols] = jnp.sum(jnp.where(own, prob * dp_ref[b, :, cols], 0.0), axis=0, keepdims=True)
        prob = jnp.where(own, 0.0, prob)
        high = prob.astype(jnp.bfloat16)
        splits.append((high, (prob - high.astype(jnp.float32)).astype(jnp.bfloat16)))
    for (b, heads, _, _), (high, low) in zip(parts, splits):
        for n, h in enumerate(heads):
            part = slice(n * rows, (n + 1) * rows)
            grad = do_ref[b, :, h * HEAD:(h + 1) * HEAD]
            g_ref[b, :, h * HEAD:(h + 1) * HEAD] = dot(
                jnp.concatenate([high[:, part], low[:, part]], axis=1), jnp.concatenate([grad, grad], axis=0),
                ((1,), (0,)))


def terms_kernel(do_ref, hv_ref, g_ref, own_ref, p_ref, dp_ref, terms_out, gp_ref, sink_ref, terms_ref, sem):
    _, rows, _ = do_ref.shape
    own = own_mask(rows, GROUP * rows)
    parts = list(groups(do_ref))
    for b, heads, kv, _ in parts:
        value = hv_ref[b, :, kv].astype(jnp.float32)
        for h in heads:
            term = jnp.sum(value * g_ref[b, :, h * HEAD:(h + 1) * HEAD], axis=0, keepdims=True)
            term += own_ref[b, :, h * rows:(h + 1) * rows]
            sink_ref[h:h + 1, :] = term if b == 0 else sink_ref[h:h + 1, :] + term
    terms = sink_ref[...]
    high = terms.astype(jnp.bfloat16)
    rest = terms - high.astype(jnp.float32)
    middle = rest.astype(jnp.bfloat16)
    low = (rest - middle.astype(jnp.float32)).astype(jnp.bfloat16)
    split_terms = jnp.concatenate([low, middle, high], axis=1)
    ones = jnp.ones((terms_ref.shape[0], split_terms.shape[1]), jnp.bfloat16)
    terms_ref[...] = dot(ones, split_terms, ((1,), (1,)))
    copy = pltpu.make_async_copy(terms_ref, terms_out, sem)
    copy.start()
    for b, heads, kv, cols in parts:
        before = dot(hv_ref[b, :, kv], stacked(do_ref, b, heads), ((1,), (1,)))
        grad_prob = jnp.where(own, dp_ref[b, :, cols], before)
        gp_ref[b, :rows, cols] = grad_prob
        gp_ref[b, rows:rows + 1, cols] = jnp.sum(
            p_ref[b, :, cols].astype(jnp.float32) * grad_prob, axis=0, keepdims=True)
    copy.wait()


def keys_kernel(q_ref, p_ref, gp_ref, ds_ref, back_ref):
    _, rows, _ = q_ref.shape
    own = own_mask(rows, GROUP * rows)
    parts = list(groups(q_ref))
    dscores = []
    for b, _, _, cols in parts:
        delta = gp_ref[b, rows:rows + 1, cols]
        dscores.append((p_ref[b, :, cols].astype(jnp.float32) * (gp_ref[b, :rows, cols] - delta)).astype(jnp.bfloat16))
        ds_ref[b, :, cols] = dscores[-1]
    for (b, heads, kv, cols), dscore in zip(parts, dscores):
        grad_key = dot(split(own, dscore)[rows:], stacked(q_ref, b, heads), ((1,), (0,))) * SCALE
        back_ref[b, :, kv] = grad_key.astype(jnp.bfloat16)


def query_kernel(q_ref, k_ref, hk_ref, ds_ref, dq_ref, dk_ref):
    _, rows, _ = dq_ref.shape
    own = own_mask(rows, GROUP * rows)
    parts = list(groups(dq_ref))
    dscores = [split(own, ds_ref[b, :, cols]) for b, _, _, cols in parts]
    for (b, heads, kv, _), dscore in zip(parts, dscores):
        dk_ref[b, :, kv] = dot(dscore[:rows], stacked(q_ref, b, heads), ((1,), (0,))) * SCALE
    keys = [jnp.concatenate([k_ref[b, :, kv], hk_ref[b, :, kv]], axis=0) for b, _, kv, _ in parts]
    products = [dot(dscore, key, ((0,), (0,))) for dscore, key in zip(dscores, keys)]
    for (b, heads, _, _), product in zip(parts, products):
        for n, h in enumerate(heads):
            dq_ref[b, :, h * HEAD:(h + 1) * HEAD] = (product[n * rows:(n + 1) * rows] * SCALE).astype(jnp.bfloat16)


def values_kernel(do_ref, p_ref, back_ref, out_ref):
    _, rows, _ = do_ref.shape
    own = own_mask(rows, GROUP * rows)
    for b, heads, kv, cols in groups(do_ref):
        prob = split(own, p_ref[b, :, cols])[:rows]
        grad_value = dot(prob, stacked(do_ref, b, heads), ((1,), (0,)))
        out_ref[b, :, kv] = (grad_value + back_ref[b, :, kv].astype(jnp.float32)).astype(jnp.bfloat16)


def total_kernel(factor, terms_ref, *refs):
    total_ref = refs[-1]
    total_ref[...] = jnp.sum(terms_ref[...], axis=0, keepdims=True) * factor


def finish_kernel(own_ref, back_ref, total_ref, out_ref, sink_ref):
    out_ref[...] = (own_ref[...] + back_ref[...].astype(jnp.float32)).astype(jnp.bfloat16)
    sink_ref[...] = total_ref[...]


def ring(value, axis, steps):
    count = lax.axis_size(axis)
    return lax.ppermute(value, axis, [(i, (i + steps) % count) for i in range(count)])


def shift(value, axis):
    count = lax.axis_size(axis)
    return lax.ppermute(value, axis, [(i, i + 1) for i in range(count - 1)])


def body(queries, keys, values, dout, sinks):
    batch, rows, width = queries.shape
    kv_width = keys.shape[2]
    dp, ctx = lax.axis_size("dp"), lax.axis_size("ctx")
    assert rows == WINDOW
    bf16, f32 = jnp.bfloat16, jnp.float32
    square = struct((batch, rows, HEADS * rows), f32)
    line = struct((batch, 1, HEADS * rows), f32)
    kv_bf16 = struct((batch, rows, kv_width), bf16)
    product = 2 * batch * HEADS * rows * rows * HEAD

    first = (lax.axis_index("ctx") == 0).astype(jnp.int32).reshape(1)
    halo_keys = ring(keys, "ctx", 1)
    halo_values = shift(values, "ctx")
    q, k, do, score, grad_prob, bias, sink = call(
        load_kernel, "load",
        (struct(queries.shape, bf16), kv_bf16, struct(dout.shape, bf16), square, square,
         struct((1, GROUP * rows), f32), struct((1, HEADS * rows), f32)),
        [SMEM] + [HBM] * 5, (first, sinks, queries, keys, values, dout), 2 * product,
        scratch=[pltpu.VMEM(values.shape, bf16), pltpu.SMEM((HEADS,), f32), pltpu.SemaphoreType.DMA((5,))])
    prob, back_values, halves, own_terms = call(
        softmax_kernel, "softmax",
        (pltpu.VMEM(square.shape, bf16), pltpu.VMEM(keys.shape, bf16),
         pltpu.VMEM(square.shape, f32), pltpu.VMEM(line.shape, f32)),
        [VMEM] * 7, (bias, sink, q, do, halo_keys, score, grad_prob), 4 * product,
        scratch=[pltpu.VMEM(square.shape, f32)])
    back_values = ring(back_values, "ctx", -1)
    terms, grad_prob = call(
        terms_kernel, "terms", (pltpu.HBM((dp * ctx, HEADS), f32), pltpu.VMEM((batch, rows + 8, HEADS * rows), f32)),
        [VMEM] * 6, (do, halo_values, halves, own_terms, prob, grad_prob), product,
        scratch=[pltpu.VMEM((HEADS, rows), f32), pltpu.VMEM((dp * ctx, HEADS), f32), pltpu.SemaphoreType.DMA],
        out_specs=(HBM, VMEM))
    dscores, back_keys = call(
        keys_kernel, "keys",
        (pltpu.VMEM(square.shape, bf16), pltpu.VMEM(keys.shape, bf16)),
        [VMEM] * 3, (q, prob, grad_prob), 2 * product)
    back_keys = ring(back_keys, "ctx", -1)
    terms = lax.all_to_all(terms, ("ctx", "dp"), 0, 0, tiled=True)
    grad_query, own_keys = call(
        query_kernel, "query", (struct(queries.shape, bf16), pltpu.VMEM(keys.shape, f32)), [VMEM] * 4,
        (q, k, halo_keys, dscores), 3 * product)
    grad_values, = call(values_kernel, "values", (kv_bf16,), [VMEM] * 3, (do, prob, back_values), product)
    factor = -1.0 / (dp * batch * ctx * rows) ** 0.5
    total, = call(
        functools.partial(total_kernel, factor), "total", (struct((1, HEADS), f32),), [VMEM, HBM, HBM],
        (terms, grad_values, grad_query), 10 ** 10)
    grad_keys, sink_grad = call(
        finish_kernel, "finish", (kv_bf16, struct((1, HEADS), f32)), [VMEM] * 3, (own_keys, back_keys, total), 0)
    return grad_query, grad_keys, grad_values, sink_grad.reshape(HEADS)


def solution(mesh):
    whole = P("dp", "ctx", None)
    return jax.shard_map(
        body,
        mesh=mesh,
        in_specs=(whole, whole, whole, whole, P()),
        out_specs=(whole, whole, whole, P()),
        check_vma=False,
    )
```
